32 devices in a mesh: slide: 4 (over x, core), space: 8 (over z, y).
Axes of the slice: x: 2, y: 2, z: 4, core: 2. Of those that a mesh axis runs over, the one named last changes fastest.
Arguments:
- features: bfloat16 [4, 8, 8, 256, 192], P('slide', 'space'), may hold values from -16 to 16
- dw_kernel: float32 [7, 7, 192], replicated, may hold values from -1.3 to 1.3
- dw_bias: float32 [192], replicated, may hold values from -4 to 4
- ln_gain: float32 [192], replicated, may hold values from 0.5 to 1.5
- ln_bias: float32 [192], replicated, may hold values from -3 to 3
- w_in: bfloat16 [192, 768], replicated, may hold values from -0.4375 to 0.4375
- b_in: float32 [768], replicated, may hold values from -3 to 3
- w_out: bfloat16 [768, 192], replicated, may hold values from -0.21875 to 0.21875
- b_out: float32 [192], replicated, may hold values from -3 to 3
- layer_scale: float32 [192], replicated, may hold values from 0.5 to 1.5
- cotangent: bfloat16 [4, 8, 8, 256, 192], P('slide', 'space'), may hold values from -6 to 6
Outputs:
- block_output: bfloat16 [4, 8, 8, 256, 192], P('slide', 'space')
- grad_input: bfloat16 [4, 8, 8, 256, 192], P('slide', 'space')
- grad_w_in: float32 [192, 768], replicated
- grad_w_out: float32 [768, 192], replicated
- grad_kernel: float32 [7, 7, 192], replicated
The draws below stay inside these ranges and needn't reach their ends.
All inputs are finite; a program needn't handle non-finite values.
Results may differ from the reference program's by a relative error of at most 0.0068.
Values may be sent and summed in bfloat16 or wider, within the bound.
No kernel may reach another device: no remote copies, remote signals or barrier semaphores. Data moves between devices by JAX's collectives and lax.ppermute only.
A program may use at most 64 MiB of HBM per device.

```python
import math
import jax
import jax.numpy as jnp
from jax import lax

C = 192
F = 768
TH = 8
TW = 256
TILES = 8
SLIDES = 4
PIXELS = 65536


def draw_features(key, part):
    shape = (SLIDES, TILES, TH, TW, C)
    first, second = jax.random.split(jax.random.fold_in(key, 11), 2)
    pixel_scale = jnp.exp(jax.random.uniform(second, (SLIDES, TILES, TH, TW, 1), jnp.float32, math.log(0.4), math.log(4.0)))
    values = jax.random.truncated_normal(first, -4.0, 4.0, shape, jnp.float32)
    return (values * pixel_scale).astype(jnp.bfloat16)


def draw_dw_kernel(key, part):
    first, second = jax.random.split(jax.random.fold_in(key, 23), 2)
    channel_scale = jnp.exp(jax.random.uniform(second, (1, 1, C), jnp.float32, math.log(0.3), math.log(3.0)))
    values = jax.random.truncated_normal(first, -3.0, 3.0, (7, 7, C), jnp.float32)
    return values * channel_scale / 7.0


def levels(stream_key, extent, cuts, least, high):
    gain, own = 1.0, jax.random.fold_in(stream_key, 6)
    for axis_at, shards_of in cuts:
        heights = jnp.exp(jax.random.uniform(jax.random.fold_in(own, axis_at), (shards_of,), jnp.float32, least / len(cuts), high / len(cuts)))
        gain = gain * jnp.repeat(heights, extent[axis_at] // shards_of).reshape([-1 if axis == axis_at else 1 for axis in range(len(extent))])
    return gain


def scatter_about(rng, extent, spread, most, cuts=(), dtype=jnp.bfloat16):
    values = spread * jax.random.normal(rng, extent, jnp.float32)
    if cuts:
        values = values * levels(rng, extent, cuts, -0.22, 0.18)
    return jnp.clip(values, -most, most).astype(dtype)


def setup_inputs(seed: int = 0) -> dict:
    splits = jax.random.split(jax.random.key(seed), 12)
    features = draw_features(jax.random.fold_in(splits[11], 71), 0)
    dw_kernel = draw_dw_kernel(jax.random.fold_in(splits[11], 71), 0)
    dw_bias = scatter_about(splits[2], (C,), 1.0, 4.0, (), jnp.float32)
    ln_gain = jnp.clip(jax.random.uniform(splits[3], (C,), jnp.float32, 0.5, 1.5), 0.5, 1.5)
    ln_bias = scatter_about(splits[4], (C,), 0.5, 3.0, (), jnp.float32)
    w_in = scatter_about(splits[5], (C, F), C ** -0.5, 0.4375)
    b_in = scatter_about(splits[6], (F,), 0.5, 3.0, (), jnp.float32)
    w_out = scatter_about(splits[7], (F, C), F ** -0.5, 0.21875)
    b_out = scatter_about(splits[8], (C,), 0.5, 3.0, (), jnp.float32)
    layer_scale = jnp.clip(jax.random.uniform(splits[9], (C,), jnp.float32, 0.5, 1.5), 0.5, 1.5)
    cotangent = scatter_about(splits[10], (SLIDES, TILES, TH, TW, C), 1.0, 6.0, ((0, 4), (1, 8)))
    return dict(features=features, dw_kernel=dw_kernel, dw_bias=dw_bias, ln_gain=ln_gain, ln_bias=ln_bias, w_in=w_in, b_in=b_in, w_out=w_out, b_out=b_out, layer_scale=layer_scale, cotangent=cotangent)


EPSILON = 1e-06

def gelu_slope(hidden):
    return 0.5 * (1.0 + lax.erf(hidden * 0.7071067811865476)) + hidden * jnp.exp(-0.5 * hidden * hidden) * 0.3989422804014327

def reference(features, dw_kernel, dw_bias, ln_gain, ln_bias, w_in, b_in, w_out, b_out, layer_scale, cotangent):
    chans = features.shape[4]
    strips, strip_rows, strip_cols = (features.shape[1], features.shape[2], features.shape[3])

    def one_slide(pair):
        image = pair[0].reshape(strips * strip_rows, strip_cols, chans).astype(jnp.float32)
        upstream = pair[1].reshape(strips * strip_rows, strip_cols, chans).astype(jnp.float32)
        height, width = (image.shape[0], image.shape[1])
        padded = jnp.pad(image, ((3, 3), (3, 3), (0, 0)))
        mixed = jnp.zeros((height, width, chans), jnp.float32) + dw_bias
        for row_off in range(7):
            for col_off in range(7):
                mixed = mixed + dw_kernel[row_off, col_off] * padded[row_off:row_off + height, col_off:col_off + width]
        flat = mixed.reshape(height * width, chans)
        centre = flat - lax.optimization_barrier(jnp.mean(flat, axis=1, keepdims=True))
        inverse = lax.rsqrt(lax.optimization_barrier(jnp.mean(centre * centre, axis=1, keepdims=True)) + EPSILON)
        unit = centre * inverse
        normed = (unit * ln_gain + ln_bias).astype(jnp.bfloat16)
        hidden = jnp.dot(normed, w_in, preferred_element_type=jnp.float32) + b_in
        act = jax.nn.gelu(hidden, approximate=False).astype(jnp.bfloat16)
        branch = jnp.dot(act, w_out, preferred_element_type=jnp.float32) + b_out
        result = (image.reshape(height * width, chans) + layer_scale * branch).astype(jnp.bfloat16)
        up_flat = upstream.reshape(height * width, chans)
        gout = (layer_scale * up_flat).astype(jnp.bfloat16)
        grad_act = jnp.dot(gout, w_out.T, preferred_element_type=jnp.float32)
        grad_hidden = (grad_act * gelu_slope(hidden)).astype(jnp.bfloat16)
        grad_norm = jnp.dot(grad_hidden, w_in.T, preferred_element_type=jnp.float32) * ln_gain
        grad_mixed = inverse * (grad_norm - lax.optimization_barrier(jnp.mean(grad_norm, axis=1, keepdims=True)) - unit * lax.optimization_barrier(jnp.mean(grad_norm * unit, axis=1, keepdims=True)))
        grad_mixed = grad_mixed.astype(jnp.bfloat16).reshape(height, width, chans)
        grad_wide = jnp.pad(grad_mixed.astype(jnp.float32), ((3, 3), (3, 3), (0, 0)))
        grad_image = upstream
        kernel_terms = []
        for row_off in range(7):
            for col_off in range(7):
                grad_image = grad_image + dw_kernel[row_off, col_off] * grad_wide[6 - row_off:6 - row_off + height, 6 - col_off:6 - col_off + width]
                kernel_terms.append(lax.optimization_barrier(jnp.sum(grad_wide[3:3 + height, 3:3 + width] * padded[row_off:row_off + height, col_off:col_off + width], axis=(0, 1))))
        grad_k = jnp.stack(kernel_terms).reshape(7, 7, chans)
        grad_wi = jnp.dot(normed.T, grad_hidden, preferred_element_type=jnp.float32)
        grad_wo = jnp.dot(act.T, gout, preferred_element_type=jnp.float32)
        out_tiles = result.reshape(strips, strip_rows, strip_cols, chans)
        grad_tiles = grad_image.astype(jnp.bfloat16).reshape(strips, strip_rows, strip_cols, chans)
        return (out_tiles, grad_tiles, grad_wi, grad_wo, grad_k)
    results = lax.map(one_slide, (features, cotangent))
    scale = jnp.float32(float(PIXELS) ** (-0.5))
    return (results[0], results[1], lax.optimization_barrier(jnp.sum(results[2], axis=0)) * scale, lax.optimization_barrier(jnp.sum(results[3], axis=0)) * scale, lax.optimization_barrier(jnp.sum(results[4], axis=0)) * scale)
```

```python
import jax
import jax.numpy as jnp
from jax import lax
from jax.experimental import pallas as pl
from jax.experimental.pallas import tpu as pltpu
from jax.sharding import PartitionSpec as P

EPSILON = 1e-06
TAPS = 7
REACH = 3
GROUP = 16
BF16 = jnp.bfloat16
F32 = jnp.float32


def shifted(value, axis, steps):
    count = lax.axis_size(axis)
    initial, last = (max(0, -steps), min(count, count - steps))
    return lax.ppermute(value, axis, [(source, source + steps) for source in range(initial, last)])


def slide_lanes(value, steps):
    if steps == 0:
        return value
    width = value.shape[-1]
    lane = lax.broadcasted_iota(jnp.int32, value.shape, value.ndim - 1)
    moved = pltpu.roll(value, (-steps) % width, value.ndim - 1)
    keep = lane < width - steps if steps > 0 else lane >= -steps
    return jnp.where(keep, moved, jnp.zeros_like(moved))


def conv_row(tall_ref, taps_ref, row):
    _, chans, width = tall_ref.shape
    pieces = []
    for group in range(chans // GROUP):
        window = tall_ref[pl.ds(row, TAPS), group * GROUP : (group + 1) * GROUP, :]
        window = window.reshape(TAPS * GROUP, width)
        parts = jnp.dot(taps_ref[group], window, preferred_element_type=F32)
        total = None
        for tap in range(TAPS):
            part = slide_lanes(parts[tap * GROUP : (tap + 1) * GROUP], tap - REACH)
            total = part if total is None else total + part
        pieces.append(total)
    return jnp.concatenate(pieces, axis=0)


def block_kernel(
    x_ref, above_ref, below_ref, g_ref, taps_ref, vec_ref, bin_ref, win_ref, wint_ref, wout_ref, woutt_ref,
    out_ref, gz_ref, terms_ref,
    tall_ref, normed_ref, act_ref, gout_ref, gh_ref,
    *, scale,
):
    rows, chans, width = x_ref.shape
    hidden_units = win_ref.shape[1]
    tall_ref[0:REACH] = above_ref[...]
    tall_ref[REACH : REACH + rows] = x_ref[...]
    tall_ref[REACH + rows :] = below_ref[...]

    def one_row(row, carry):
        def vec(index):
            return vec_ref[:, index : index + 1]

        mixed = conv_row(tall_ref, taps_ref, row) + vec(0)
        centre = mixed - jnp.mean(mixed, axis=0, keepdims=True)
        inverse = lax.rsqrt(jnp.mean(centre * centre, axis=0, keepdims=True) + EPSILON)
        unit = centre * inverse
        normed = (unit * vec(1) + vec(2)).astype(BF16)
        normed_ref[row] = normed
        gout = (vec(4) * g_ref[row].astype(F32)).astype(BF16)
        gout_ref[row] = gout
        span = 256
        for start in range(0, hidden_units, span):
            part = slice(start, start + span)
            hidden = jnp.dot(wint_ref[part, :], normed, preferred_element_type=F32) + bin_ref[part, :]
            grad_act = jnp.dot(wout_ref[part, :], gout, preferred_element_type=F32)
            cdf = 0.5 * (1.0 + lax.erf(hidden * 0.7071067811865476))
            slope = cdf + hidden * jnp.exp(-0.5 * hidden * hidden) * 0.3989422804014327
            act_ref[row, part, :] = (hidden * cdf).astype(BF16)
            gh_ref[row, part, :] = (grad_act * slope).astype(BF16)
        branch = jnp.dot(woutt_ref[...], act_ref[row], preferred_element_type=F32) + vec(3)
        out_ref[row] = (x_ref[row].astype(F32) + vec(4) * branch).astype(BF16)
        grad_norm = jnp.dot(win_ref[...], gh_ref[row], preferred_element_type=F32) * vec(1)
        grad_mixed = inverse * (
            grad_norm
            - jnp.mean(grad_norm, axis=0, keepdims=True)
            - unit * jnp.mean(grad_norm * unit, axis=0, keepdims=True)
        )
        gz_ref[row] = grad_mixed.astype(BF16)
        return carry

    lax.fori_loop(0, rows, one_row, 0)

    nt = (((1,), (1,)), ((), ()))
    blocks = hidden_units // 128
    for index, (left, right) in enumerate(((normed_ref, gh_ref), (gout_ref, act_ref))):
        for start in range(0, hidden_units, 256):
            total = None
            for row in range(rows):
                term = lax.dot_general(left[row], right[row, start : start + 256, :], nt, preferred_element_type=F32)
                total = term if total is None else total + term
            for lanes in range(2):
                block = start // 128 + lanes
                terms_ref[index, block * chans : (block + 1) * chans, :] = (
                    total[:, lanes * 128 : (lanes + 1) * 128] * scale
                ).astype(BF16)
    taps_at = blocks * chans
    span = TAPS * GROUP
    same = lax.broadcasted_iota(jnp.int32, (span, span), 0) % GROUP == lax.broadcasted_iota(
        jnp.int32, (span, span), 1
    ) % GROUP
    groups = chans // GROUP
    terms_ref[:, taps_at:, :] = jnp.zeros((2, terms_ref.shape[1] - taps_at, 128), BF16)
    for group in range(groups):
        total = None
        for row in range(rows):
            grad = gz_ref[row, group * GROUP : (group + 1) * GROUP, :].astype(F32)
            moved = jnp.concatenate([slide_lanes(grad, REACH - tap) for tap in range(TAPS)], axis=0).astype(BF16)
            window = tall_ref[row : row + TAPS, group * GROUP : (group + 1) * GROUP, :].reshape(span, width)
            term = lax.dot_general(moved, window, nt, preferred_element_type=F32)
            total = term if total is None else total + term
        total = jnp.where(same, total, 0.0) * scale
        summed = jnp.sum(total.reshape(TAPS, GROUP, span), axis=1)
        summed = jnp.concatenate([summed, jnp.zeros((1, span), F32)], axis=0)
        summed = jnp.concatenate([summed, jnp.zeros((8, 128 - span), F32)], axis=1)
        half, place = divmod(group, groups // 2)
        terms_ref[half, taps_at + place * 16 : taps_at + place * 16 + 8, :] = summed.astype(BF16)


def input_kernel(gz_ref, above_ref, below_ref, g_ref, taps_ref, out_ref, tall_ref):
    rows, chans, width = gz_ref.shape
    tall_ref[0:REACH] = above_ref[...]
    tall_ref[REACH : REACH + rows] = gz_ref[...]
    tall_ref[REACH + rows :] = below_ref[...]

    def one_row(row, carry):
        out_ref[row] = (g_ref[row].astype(F32) + conv_row(tall_ref, taps_ref, row)).astype(BF16)
        return carry

    lax.fori_loop(0, rows, one_row, 0)


def final_kernel(sum_ref, win_ref, woutt_ref, taps_ref):
    chans, hidden_units = win_ref.shape
    blocks = hidden_units // 128
    for index, ref in enumerate((win_ref, woutt_ref)):
        for block in range(blocks):
            ref[:, block * 128 : (block + 1) * 128] = sum_ref[index, block * chans : (block + 1) * chans, :].astype(F32)
    groups = chans // GROUP
    for group in range(groups):
        half, place = divmod(group, groups // 2)
        at = blocks * chans + place * 16
        piece = sum_ref[half, at : at + 16, :].astype(F32)[:8]
        for tap in range(TAPS):
            taps_ref[tap, :, group * GROUP : (group + 1) * GROUP] = piece[:TAPS, tap * GROUP : (tap + 1) * GROUP]


def spread(kernel):
    chans = kernel.shape[2]
    groups = chans // GROUP
    by_group = kernel.reshape(TAPS, TAPS, groups, GROUP).transpose(2, 1, 3, 0)
    eye = jnp.eye(GROUP, dtype=F32)
    wide = by_group[..., None] * eye[None, None, :, None, :]
    return wide.reshape(groups, TAPS * GROUP, TAPS * GROUP).astype(BF16)


VMEM_LIMIT = pltpu.CompilerParams(vmem_limit_bytes=48 * 1024 * 1024)


def on_device(
    features, dw_kernel, dw_bias, ln_gain, ln_bias, w_in, b_in, w_out, b_out, layer_scale, cotangent
):
    x = jnp.swapaxes(features[0, 0], 1, 2)
    g = jnp.swapaxes(cotangent[0, 0], 1, 2)
    rows, chans, width = x.shape
    hidden_units = w_in.shape[1]
    above = shifted(x[-REACH:], "space", 1)
    below = shifted(x[:REACH], "space", -1)
    taps = spread(dw_kernel)
    back_taps = spread(dw_kernel[::-1, ::-1])
    vectors = jnp.stack([dw_bias, ln_gain, ln_bias, b_out, layer_scale], axis=1)
    devices = lax.axis_size("slide") * lax.axis_size("space")
    scale = float(devices * rows * width) ** (-0.5)
    chunk = 16
    term_rows = hidden_units // 128 * chans + chans // GROUP * 8
    unit = 16 * (devices // 2)
    term_rows = (term_rows + unit - 1) // unit * unit
    out, gz, terms = pl.pallas_call(
        lambda *refs: block_kernel(*refs, scale=scale),
        out_shape=(
            jax.ShapeDtypeStruct((rows, chans, width), BF16),
            jax.ShapeDtypeStruct((rows, chans, width), BF16),
            jax.ShapeDtypeStruct((2, term_rows, 128), BF16),
        ),
        scratch_shapes=[
            pltpu.VMEM((rows + 2 * REACH, chans, width), BF16),
            pltpu.VMEM((rows, chans, width), BF16),
            pltpu.VMEM((rows, hidden_units, width), BF16),
            pltpu.VMEM((rows, chans, width), BF16),
            pltpu.VMEM((rows, hidden_units, width), BF16),
        ],
        compiler_params=VMEM_LIMIT,
    )(x, above, below, g, taps, vectors, b_in[:, None], w_in, w_in.T, w_out, w_out.T)
    gz_above = shifted(gz[-REACH:], "space", 1)
    gz_below = shifted(gz[:REACH], "space", -1)
    axes = ("slide", "space")
    mine = 2 * term_rows // devices
    parts = lax.all_to_all(terms.reshape(devices, mine, 128), axes, 0, 0, tiled=True)
    own = jnp.sum(parts.astype(F32), axis=0).astype(BF16)
    summed = lax.all_to_all(jnp.broadcast_to(own, (devices, mine, 128)), axes, 0, 0, tiled=True)
    grad_input = pl.pallas_call(
        input_kernel,
        out_shape=jax.ShapeDtypeStruct((rows, chans, width), BF16),
        scratch_shapes=[pltpu.VMEM((rows + 2 * REACH, chans, width), BF16)],
        compiler_params=VMEM_LIMIT,
    )(gz, gz_above, gz_below, g, back_taps)
    grad_w_in, grad_w_out_t, grad_kernel = pl.pallas_call(
        final_kernel,
        out_shape=(
            jax.ShapeDtypeStruct((chans, hidden_units), F32),
            jax.ShapeDtypeStruct((chans, hidden_units), F32),
            jax.ShapeDtypeStruct((TAPS, TAPS, chans), F32),
        ),
        compiler_params=VMEM_LIMIT,
    )(summed.reshape(2, term_rows, 128))
    block_output = jnp.swapaxes(out, 1, 2)[None, None]
    grad_image = jnp.swapaxes(grad_input, 1, 2)[None, None]
    return (block_output, grad_image, grad_w_in, grad_w_out_t.T, grad_kernel)


def solution(mesh):
    placed = P("slide", "space", None, None, None)
    return jax.shard_map(
        on_device,
        mesh=mesh,
        in_specs=(placed,) + (P(),) * 9 + (placed,),
        out_specs=(placed, placed, P(), P(), P()),
        check_vma=False,
    )
```

```python
import jax
import jax.numpy as jnp
from jax import lax
from jax.experimental import pallas as pl
from jax.experimental.pallas import tpu as pltpu
from jax.sharding import Mesh
from jax.sharding import PartitionSpec as P

EPSILON = 1e-06
TAPS = 7
REACH = 3
GROUP = 16
BF16 = jnp.bfloat16
F32 = jnp.float32


def shifted(value, axis, steps):
    count = lax.axis_size(axis)
    initial, last = (max(0, -steps), min(count, count - steps))
    return lax.ppermute(value, axis, [(source, source + steps) for source in range(initial, last)])


def slide_lanes(value, steps):
    if steps == 0:
        return value
    width = value.shape[-1]
    lane = lax.broadcasted_iota(jnp.int32, value.shape, value.ndim - 1)
    moved = pltpu.roll(value, (-steps) % width, value.ndim - 1)
    keep = lane < width - steps if steps > 0 else lane >= -steps
    return jnp.where(keep, moved, jnp.zeros_like(moved))


def conv_row(tall_ref, taps_ref, row):
    _, chans, width = tall_ref.shape
    pieces = []
    for group in range(chans // GROUP):
        window = tall_ref[pl.ds(row, TAPS), group * GROUP : (group + 1) * GROUP, :]
        window = window.reshape(TAPS * GROUP, width)
        window = jnp.concatenate([window, window], axis=0)
        parts = jnp.dot(taps_ref[group], window, preferred_element_type=F32)
        total = None
        for tap in range(TAPS):
            part = slide_lanes(parts[tap * GROUP : (tap + 1) * GROUP], tap - REACH)
            total = part if total is None else total + part
        pieces.append(total)
    return jnp.concatenate(pieces, axis=0)


def spread_taps(kernel_ref, taps_ref, flipped):
    chans = kernel_ref.shape[2]
    span = TAPS * GROUP
    same = lax.broadcasted_iota(jnp.int32, (GROUP, span), 0) == lax.broadcasted_iota(
        jnp.int32, (GROUP, span), 1
    ) % GROUP
    for group in range(chans // GROUP):
        lanes = slice(group * GROUP, (group + 1) * GROUP)
        order = [TAPS - 1 - tap if flipped else tap for tap in range(TAPS)]
        across = jnp.concatenate([kernel_ref[tap, :, lanes] for tap in order], axis=1)
        for tap in range(TAPS):
            source = TAPS - 1 - tap if flipped else tap
            wide = jnp.broadcast_to(across[source : source + 1], (GROUP, span))
            wide = jnp.where(same, wide, 0.0)
            high = wide.astype(BF16)
            low = (wide - high.astype(F32)).astype(BF16)
            taps_ref[group, tap * GROUP : (tap + 1) * GROUP, :] = jnp.concatenate([high, low], axis=1)


def one_row(row, tall_ref, g_ref, taps_ref, weights, out_ref, gz_ref, kept):
    vec_ref, bin_ref, win_ref, wint_ref, wout_ref, woutt_ref = weights
    normed_ref, act_ref, gout_ref, gh_ref = kept

    def vec(index):
        return vec_ref[:, index : index + 1]

    hidden_units = win_ref.shape[1]
    mixed = conv_row(tall_ref, taps_ref, row) + vec(0)
    centre = mixed - jnp.mean(mixed, axis=0, keepdims=True)
    inverse = lax.rsqrt(jnp.mean(centre * centre, axis=0, keepdims=True) + EPSILON)
    unit = centre * inverse
    normed = (unit * vec(1) + vec(2)).astype(BF16)
    normed_ref[row] = normed
    gout = (vec(4) * g_ref[row].astype(F32)).astype(BF16)
    gout_ref[row] = gout
    span = 256
    for start in range(0, hidden_units, span):
        part = slice(start, start + span)
        hidden = jnp.dot(wint_ref[part, :], normed, preferred_element_type=F32) + bin_ref[part, :]
        grad_act = jnp.dot(wout_ref[part, :], gout, preferred_element_type=F32)
        cdf = 0.5 * (1.0 + lax.erf(hidden * 0.7071067811865476))
        slope = cdf + hidden * jnp.exp(-0.5 * hidden * hidden) * 0.3989422804014327
        act_ref[row, part, :] = (hidden * cdf).astype(BF16)
        gh_ref[row, part, :] = (grad_act * slope).astype(BF16)
    branch = jnp.dot(woutt_ref[...], act_ref[row], preferred_element_type=F32) + vec(3)
    out_ref[row] = (tall_ref[row + REACH].astype(F32) + vec(4) * branch).astype(BF16)
    grad_norm = jnp.dot(win_ref[...], gh_ref[row], preferred_element_type=F32) * vec(1)
    grad_mixed = inverse * (
        grad_norm
        - jnp.mean(grad_norm, axis=0, keepdims=True)
        - unit * jnp.mean(grad_norm * unit, axis=0, keepdims=True)
    )
    gz_ref[row] = grad_mixed.astype(BF16)


def all_rows(tall_ref, g_ref, taps_ref, weights, out_ref, gz_ref, kept):
    def step(row, carry):
        one_row(row, tall_ref, g_ref, taps_ref, weights, out_ref, gz_ref, kept)
        return carry

    lax.fori_loop(0, out_ref.shape[0], step, 0)


NT = (((1,), (1,)), ((), ()))


def total_of(terms):
    total = terms[0]
    for term in terms[1:]:
        total = total + term
    return total


def weight_terms(kept, start, width, index):
    normed_ref, act_ref, gout_ref, gh_ref = kept
    left, right = ((normed_ref, gh_ref), (gout_ref, act_ref))[index]
    return total_of(
        [
            lax.dot_general(left[row], right[row, start : start + width, :], NT, preferred_element_type=F32)
            for row in range(left.shape[0])
        ]
    )


def tap_terms(tall_ref, gz_ref, group):
    span = TAPS * GROUP
    same = lax.broadcasted_iota(jnp.int32, (span, span), 0) % GROUP == lax.broadcasted_iota(
        jnp.int32, (span, span), 1
    ) % GROUP
    lanes = slice(group * GROUP, (group + 1) * GROUP)
    terms = []
    for row in range(gz_ref.shape[0]):
        grad = gz_ref[row, lanes, :].astype(F32)
        moved = jnp.concatenate([slide_lanes(grad, REACH - tap) for tap in range(TAPS)], axis=0).astype(BF16)
        window = tall_ref[row : row + TAPS, lanes, :].reshape(span, -1)
        terms.append(lax.dot_general(moved, window, NT, preferred_element_type=F32))
    total = jnp.where(same, total_of(terms), 0.0)
    summed = jnp.sum(total.reshape(TAPS, GROUP, span), axis=1)
    return jnp.concatenate([summed, jnp.zeros((1, span), F32)], axis=0)


def inner_kernel(
    x_ref, g_ref, kernel_ref, vec_ref, bin_ref, win_ref, wint_ref, wout_ref, woutt_ref,
    taps_ref, back_ref, out_ref, gz_ref, dwin_ref, dwout_ref, dtaps_ref,
    *kept,
):
    hidden_units = win_ref.shape[1]
    spread_taps(kernel_ref, taps_ref, False)
    spread_taps(kernel_ref, back_ref, True)
    weights = (vec_ref, bin_ref, win_ref, wint_ref, wout_ref, woutt_ref)
    all_rows(x_ref, g_ref.at[pl.ds(REACH, out_ref.shape[0])], taps_ref, weights, out_ref, gz_ref, kept)
    for start in range(0, hidden_units, 256):
        for index, ref in enumerate((dwin_ref, dwout_ref)):
            ref[:, start : start + 256] = weight_terms(kept, start, 256, index)
    for group in range(x_ref.shape[1] // GROUP):
        dtaps_ref[group] = tap_terms(x_ref, gz_ref, group)


def upper_kernel(
    x_ref, above_ref, g_ref, taps_ref, vec_ref, bin_ref, win_ref, wint_ref, wout_ref, woutt_ref,
    dwin_in_ref, dwout_in_ref, dtaps_in_ref,
    out_ref, gz_ref, dwin_ref, dwout_ref, dtaps_ref,
    tall_ref, *kept,
):
    hidden_units = win_ref.shape[1]
    tall_ref[0:REACH] = above_ref[...]
    tall_ref[REACH:] = x_ref[0 : 2 * REACH]
    weights = (vec_ref, bin_ref, win_ref, wint_ref, wout_ref, woutt_ref)
    all_rows(tall_ref, g_ref.at[pl.ds(0, REACH)], taps_ref, weights, out_ref, gz_ref, kept)
    for start in range(0, hidden_units, 256):
        part = slice(start, start + 256)
        for index, (ref, before_ref) in enumerate(((dwin_ref, dwin_in_ref), (dwout_ref, dwout_in_ref))):
            ref[:, part] = weight_terms(kept, start, 256, index) + before_ref[:, part]
    for group in range(x_ref.shape[1] // GROUP):
        dtaps_ref[group] = tap_terms(tall_ref, gz_ref, group) + dtaps_in_ref[group]


def lower_kernel(
    x_ref, below_ref, g_ref, taps_ref, vec_ref, bin_ref, win_ref, wint_ref, wout_ref, woutt_ref,
    out_ref, gz_ref, tall_ref, *kept,
):
    rows = x_ref.shape[0]
    tall_ref[0 : 2 * REACH] = x_ref[rows - 2 * REACH :]
    tall_ref[2 * REACH :] = below_ref[...]
    weights = (vec_ref, bin_ref, win_ref, wint_ref, wout_ref, woutt_ref)
    all_rows(tall_ref, g_ref.at[pl.ds(rows - REACH, REACH)], taps_ref, weights, out_ref, gz_ref, kept)


def terms_kernel(
    core_ref, tall_ref, gz_ref, normed_ref, act_ref, gout_ref, gh_ref, dwin_ref, dwout_ref, dtaps_ref,
    keep_ref, send_ref, halves_ref, *, scale,
):
    chans, hidden_units = dwin_ref.shape
    kept = (normed_ref, act_ref, gout_ref, gh_ref)
    blocks = hidden_units // 128
    for index, ref in enumerate((dwin_ref, dwout_ref)):
        for start in range(0, hidden_units, 256):
            total = (weight_terms(kept, start, 256, index) + ref[:, start : start + 256]) * scale
            for lanes in range(2):
                block = start // 128 + lanes
                halves_ref[index, block * chans : (block + 1) * chans, :] = total[
                    :, lanes * 128 : (lanes + 1) * 128
                ].astype(BF16)
    at = blocks * chans
    groups = chans // GROUP
    halves_ref[:, at:, :] = jnp.zeros((2, halves_ref.shape[1] - at, 128), BF16)
    span = TAPS * GROUP
    for pair in range(groups // 2):
        both = [
            (tap_terms(tall_ref, gz_ref, group) + dtaps_ref[group]) * scale for group in (2 * pair, 2 * pair + 1)
        ]
        both = jnp.concatenate(both, axis=0)
        both = jnp.concatenate([both, jnp.zeros((16, 128 - span), F32)], axis=1)
        half, place = divmod(pair, groups // 4)
        halves_ref[half, at + place * 16 : at + (place + 1) * 16, :] = both.astype(BF16)
    core = core_ref[0]
    keep_ref[...] = halves_ref[core]
    send_ref[...] = halves_ref[1 - core]


def input_kernel(
    out_upper_ref, out_inner_ref, out_lower_ref, gz_upper_ref, gz_inner_ref, gz_lower_ref,
    above_ref, below_ref, g_ref, taps_ref,
    out_ref, grad_ref, tall_ref,
):
    rows = g_ref.shape[0]
    at = 0
    for ref in (above_ref, gz_upper_ref, gz_inner_ref, gz_lower_ref, below_ref):
        tall_ref[at : at + ref.shape[0]] = ref[...]
        at += ref.shape[0]
    at = 0
    for ref in (out_upper_ref, out_inner_ref, out_lower_ref):
        out_ref[at : at + ref.shape[0]] = ref[...]
        at += ref.shape[0]

    def step(row, carry):
        grad_ref[row] = (g_ref[row].astype(F32) + conv_row(tall_ref, taps_ref, row)).astype(BF16)
        return carry

    lax.fori_loop(0, rows, step, 0)


def final_kernel(place_ref, mine_ref, other_ref, win_ref, woutt_ref, taps_ref, all_ref):
    core, quarter = place_ref[0], place_ref[1]
    chans, hidden_units = win_ref.shape
    size = mine_ref.shape[1]
    for turn in range(4):
        at = pl.ds(pl.multiple_of((quarter ^ turn) * size, 16), size)
        all_ref[core, at, :] = mine_ref[turn]
        all_ref[1 - core, at, :] = other_ref[turn]
    blocks = hidden_units // 128
    for index, ref in enumerate((win_ref, woutt_ref)):
        for block in range(blocks):
            ref[:, block * 128 : (block + 1) * 128] = all_ref[index, block * chans : (block + 1) * chans, :].astype(F32)
    groups = chans // GROUP
    for pair in range(groups // 2):
        half, place = divmod(pair, groups // 4)
        at = blocks * chans + place * 16
        both = all_ref[half, at : at + 16, :].astype(F32)
        for side in range(2):
            group = 2 * pair + side
            piece = both[side * 8 : side * 8 + 8]
            for tap in range(TAPS):
                taps_ref[tap, :, group * GROUP : (group + 1) * GROUP] = piece[:TAPS, tap * GROUP : (tap + 1) * GROUP]


def edge_kernel(x_ref, edge_ref, sem, *, start):
    copy = pltpu.make_async_copy(x_ref.at[pl.ds(start, REACH)], edge_ref, sem)
    copy.start()
    copy.wait()


PARAMS = pltpu.CompilerParams(vmem_limit_bytes=20 * 1024 * 1024)
SMALL = pltpu.CompilerParams(vmem_limit_bytes=4 * 1024 * 1024)
IN_VMEM = pl.BlockSpec(memory_space=pltpu.VMEM)
IN_SMEM = pl.BlockSpec(memory_space=pltpu.SMEM)


def swap(value, axis, mask):
    count = lax.axis_size(axis)
    return lax.ppermute(value, axis, [(source, source ^ mask) for source in range(count)])


def added(*terms):
    terms = [term.astype(F32) for term in terms]
    while len(terms) > 1:
        terms = [terms[at] + terms[at + 1] for at in range(0, len(terms), 2)]
    return terms[0].astype(BF16)


def on_device(
    features, dw_kernel, dw_bias, ln_gain, ln_bias, w_in, b_in, w_out, b_out, layer_scale, cotangent
):
    core = lax.axis_index("core").astype(jnp.uint32)
    quarter = (2 * lax.axis_index("x") + lax.axis_index("space") % 2).astype(jnp.uint32)
    turns = [quarter ^ turn for turn in range(4)]
    place = jnp.stack([core, quarter]).astype(jnp.int32)
    features, place, *turns = lax.optimization_barrier((features, place, *turns))
    x = jnp.swapaxes(features[0, 0], 1, 2)
    g = jnp.swapaxes(cotangent[0, 0], 1, 2)
    rows, chans, width = x.shape
    hidden_units = w_in.shape[1]
    strips = lax.axis_size("space")
    narrow = jax.ShapeDtypeStruct((REACH, chans, width), BF16)
    image = jax.ShapeDtypeStruct((rows, chans, width), BF16)

    def edge(start):
        return pl.pallas_call(
            lambda *refs: edge_kernel(*refs, start=start),
            out_shape=narrow,
            in_specs=[pl.BlockSpec(memory_space=pl.ANY)],
            out_specs=IN_VMEM,
            scratch_shapes=[pltpu.SemaphoreType.DMA(())],
            compiler_params=SMALL,
        )(x)

    above = shifted(edge(rows - REACH), "space", 1)
    vectors = jnp.stack([dw_bias, ln_gain, ln_bias, b_out, layer_scale], axis=1)
    weights = (vectors, b_in[:, None], w_in, w_in.T, w_out, w_out.T)
    devices = lax.axis_size("x") * lax.axis_size("core") * strips
    scale = float(devices * rows * width) ** (-0.5)
    groups = chans // GROUP
    span = TAPS * GROUP
    inner = rows - 2 * REACH

    tall = jax.ShapeDtypeStruct((3 * REACH, chans, width), BF16)

    def kept(count):
        small = jax.ShapeDtypeStruct((count, chans, width), BF16)
        large = jax.ShapeDtypeStruct((count, hidden_units, width), BF16)
        return (small, large, small, large)

    def scratch(shapes):
        return [pltpu.VMEM(shape.shape, shape.dtype) for shape in shapes]

    middle = jax.ShapeDtypeStruct((inner, chans, width), BF16)
    spread = jax.ShapeDtypeStruct((groups, span, 2 * span), BF16)
    matrix = jax.ShapeDtypeStruct((chans, hidden_units), F32)
    terms = (matrix, matrix, jax.ShapeDtypeStruct((groups, 8, span), F32))
    taps, back_taps, out_inner, gz_inner, *inner_terms = pl.pallas_call(
        inner_kernel,
        out_shape=(spread, spread, middle, middle, *terms),
        in_specs=[IN_VMEM] * 9,
        out_specs=(IN_VMEM,) * 7,
        scratch_shapes=scratch(kept(inner)),
        compiler_params=PARAMS,
    )(x, g, dw_kernel, *weights)
    above, top, out_inner = lax.optimization_barrier((above, edge(0), out_inner))
    below = shifted(top, "space", -1)
    half_rows = hidden_units // 128 * chans + groups // 2 * 8
    half_rows = (half_rows + 63) // 64 * 64
    half = jax.ShapeDtypeStruct((half_rows, 128), BF16)
    out_upper, gz_upper, *upper_terms = pl.pallas_call(
        upper_kernel,
        out_shape=(narrow, narrow, *terms),
        in_specs=[IN_VMEM] * 13,
        out_specs=(IN_VMEM,) * 5,
        scratch_shapes=scratch((tall, *kept(REACH))),
        compiler_params=PARAMS,
    )(x, above, g, taps, *weights, *inner_terms)
    gz_below = shifted(gz_upper, "space", -1)
    out_lower, gz_lower, *lower_kept = pl.pallas_call(
        lower_kernel,
        out_shape=(narrow, narrow, tall, *kept(REACH)),
        in_specs=[IN_VMEM] * 10,
        out_specs=(IN_VMEM,) * 7,
        compiler_params=PARAMS,
    )(x, below, g, taps, *weights)
    gz_above = shifted(gz_lower, "space", 1)
    keep, send = pl.pallas_call(
        lambda *refs: terms_kernel(*refs, scale=scale),
        out_shape=(half, half),
        in_specs=[IN_SMEM] + [IN_VMEM] * 9,
        out_specs=(IN_VMEM,) * 2,
        scratch_shapes=[pltpu.VMEM((2, half_rows, 128), BF16)],
        compiler_params=PARAMS,
    )(place, lower_kept[0], gz_lower, *lower_kept[1:], *upper_terms)

    summed = added(keep, swap(send, "core", 1)).reshape(4, half_rows // 4, 128)

    def at(turn):
        return lax.dynamic_index_in_dim(summed, turns[turn], 0, keepdims=False)

    def partner(value, turn):
        return swap(value, ("x", "space"), (turn >> 1) * strips | (turn & 1))

    own = added(at(0), *[partner(at(turn), turn) for turn in (1, 2, 3)])
    out, grad_input = pl.pallas_call(
        input_kernel,
        out_shape=(image, image),
        in_specs=[IN_VMEM] * 10,
        out_specs=(IN_VMEM, IN_VMEM),
        scratch_shapes=[pltpu.VMEM((rows + 2 * REACH, chans, width), BF16)],
        compiler_params=PARAMS,
    )(out_upper, out_inner, out_lower, gz_upper, gz_inner, gz_lower, gz_above, gz_below, g, back_taps)
    bit = 2
    while bit < strips:
        masks = (bit, 2 * bit, 3 * bit) if 2 * bit < strips else (bit,)
        own = added(own, *[swap(own, "space", mask) for mask in masks])
        bit *= 4
    own, grad_input = lax.optimization_barrier((own, grad_input))
    mine = jnp.stack([own] + [partner(own, turn) for turn in (1, 2, 3)])
    other = swap(mine, "core", 1)
    grad_w_in, grad_w_out_t, grad_kernel = pl.pallas_call(
        final_kernel,
        out_shape=(matrix, matrix, jax.ShapeDtypeStruct((TAPS, TAPS, chans), F32)),
        in_specs=[IN_SMEM, IN_VMEM, IN_VMEM],
        out_specs=(IN_VMEM,) * 3,
        scratch_shapes=[pltpu.VMEM((2, half_rows, 128), BF16)],
        compiler_params=PARAMS,
    )(place, mine, other)
    block_output = jnp.swapaxes(out, 1, 2)[None, None]
    grad_image = jnp.swapaxes(grad_input, 1, 2)[None, None]
    return (block_output, grad_image, grad_w_in, grad_w_out_t.T, grad_kernel)


def solution(mesh):
    slides, strips = mesh.devices.shape
    split = Mesh(mesh.devices.reshape(slides // 2, 2, strips), ("x", "core", "space"))
    placed = P(("x", "core"), "space", None, None, None)
    return jax.shard_map(
        on_device,
        mesh=split,
        in_specs=(placed,) + (P(),) * 9 + (placed,),
        out_specs=(placed, placed, P(), P(), P()),
        check_vma=False,
    )
```

```python
import jax
import jax.numpy as jnp
from jax import lax
from jax.experimental import pallas as pl
from jax.experimental.pallas import tpu as pltpu
from jax.sharding import Mesh
from jax.sharding import PartitionSpec as P

EPSILON = 1e-06
TAPS = 7
REACH = 3
GROUP = 16
BF16 = jnp.bfloat16
F32 = jnp.float32


def shifted(value, axis, steps):
    count = lax.axis_size(axis)
    initial, last = (max(0, -steps), min(count, count - steps))
    return lax.ppermute(value, axis, [(source, source + steps) for source in range(initial, last)])


def slide_lanes(value, steps):
    if steps == 0:
        return value
    width = value.shape[-1]
    lane = lax.broadcasted_iota(jnp.int32, value.shape, value.ndim - 1)
    moved = pltpu.roll(value, (-steps) % width, value.ndim - 1)
    keep = lane < width - steps if steps > 0 else lane >= -steps
    return jnp.where(keep, moved, jnp.zeros_like(moved))


def conv_row(tall_ref, taps_ref, row):
    _, chans, width = tall_ref.shape
    pieces = []
    for group in range(chans // GROUP):
        window = tall_ref[pl.ds(row, TAPS), group * GROUP : (group + 1) * GROUP, :]
        window = window.reshape(TAPS * GROUP, width)
        window = jnp.concatenate([window, window], axis=0)
        parts = jnp.dot(taps_ref[group], window, preferred_element_type=F32)
        total = None
        for tap in range(TAPS):
            part = slide_lanes(parts[tap * GROUP : (tap + 1) * GROUP], tap - REACH)
            total = part if total is None else total + part
        pieces.append(total)
    return jnp.concatenate(pieces, axis=0)


def spread_taps(kernel_ref, taps_ref, flipped):
    chans = kernel_ref.shape[2]
    span = TAPS * GROUP
    same = lax.broadcasted_iota(jnp.int32, (GROUP, span), 0) == lax.broadcasted_iota(
        jnp.int32, (GROUP, span), 1
    ) % GROUP
    for group in range(chans // GROUP):
        lanes = slice(group * GROUP, (group + 1) * GROUP)
        order = [TAPS - 1 - tap if flipped else tap for tap in range(TAPS)]
        across = jnp.concatenate([kernel_ref[tap, :, lanes] for tap in order], axis=1)
        for tap in range(TAPS):
            source = TAPS - 1 - tap if flipped else tap
            wide = jnp.broadcast_to(across[source : source + 1], (GROUP, span))
            wide = jnp.where(same, wide, 0.0)
            high = wide.astype(BF16)
            low = (wide - high.astype(F32)).astype(BF16)
            taps_ref[group, tap * GROUP : (tap + 1) * GROUP, :] = jnp.concatenate([high, low], axis=1)


def one_row(row, tall_ref, g_ref, taps_ref, weights, out_ref, gz_ref, kept):
    vec_ref, bin_ref, win_ref, wint_ref, wout_ref, woutt_ref = weights
    normed_ref, act_ref, gout_ref, gh_ref = kept

    def vec(index):
        return vec_ref[:, index : index + 1]

    hidden_units = win_ref.shape[1]
    mixed = conv_row(tall_ref, taps_ref, row) + vec(0)
    centre = mixed - jnp.mean(mixed, axis=0, keepdims=True)
    inverse = lax.rsqrt(jnp.mean(centre * centre, axis=0, keepdims=True) + EPSILON)
    unit = centre * inverse
    normed = (unit * vec(1) + vec(2)).astype(BF16)
    normed_ref[row] = normed
    gout = (vec(4) * g_ref[row].astype(F32)).astype(BF16)
    gout_ref[row] = gout
    span = 256
    for start in range(0, hidden_units, span):
        part = slice(start, start + span)
        hidden = jnp.dot(wint_ref[part, :], normed, preferred_element_type=F32) + bin_ref[part, :]
        grad_act = jnp.dot(wout_ref[part, :], gout, preferred_element_type=F32)
        cdf = 0.5 * (1.0 + lax.erf(hidden * 0.7071067811865476))
        slope = cdf + hidden * jnp.exp(-0.5 * hidden * hidden) * 0.3989422804014327
        act_ref[row, part, :] = (hidden * cdf).astype(BF16)
        gh_ref[row, part, :] = (grad_act * slope).astype(BF16)
    branch = jnp.dot(woutt_ref[...], act_ref[row], preferred_element_type=F32) + vec(3)
    out_ref[row] = (tall_ref[row + REACH].astype(F32) + vec(4) * branch).astype(BF16)
    grad_norm = jnp.dot(win_ref[...], gh_ref[row], preferred_element_type=F32) * vec(1)
    grad_mixed = inverse * (
        grad_norm
        - jnp.mean(grad_norm, axis=0, keepdims=True)
        - unit * jnp.mean(grad_norm * unit, axis=0, keepdims=True)
    )
    gz_ref[row] = grad_mixed.astype(BF16)


def all_rows(tall_ref, g_ref, taps_ref, weights, out_ref, gz_ref, kept):
    def step(row, carry):
        one_row(row, tall_ref, g_ref, taps_ref, weights, out_ref, gz_ref, kept)
        return carry

    lax.fori_loop(0, out_ref.shape[0], step, 0)


NT = (((1,), (1,)), ((), ()))


def total_of(terms):
    total = terms[0]
    for term in terms[1:]:
        total = total + term
    return total


def weight_terms(kept, start, width, index):
    normed_ref, act_ref, gout_ref, gh_ref = kept
    left, right = ((normed_ref, gh_ref), (gout_ref, act_ref))[index]
    return total_of(
        [
            lax.dot_general(left[row], right[row, start : start + width, :], NT, preferred_element_type=F32)
            for row in range(left.shape[0])
        ]
    )


def tap_terms(tall_ref, gz_ref, group):
    span = TAPS * GROUP
    same = lax.broadcasted_iota(jnp.int32, (span, span), 0) % GROUP == lax.broadcasted_iota(
        jnp.int32, (span, span), 1
    ) % GROUP
    lanes = slice(group * GROUP, (group + 1) * GROUP)
    terms = []
    for row in range(gz_ref.shape[0]):
        grad = gz_ref[row, lanes, :].astype(F32)
        moved = jnp.concatenate([slide_lanes(grad, REACH - tap) for tap in range(TAPS)], axis=0).astype(BF16)
        window = tall_ref[row : row + TAPS, lanes, :].reshape(span, -1)
        terms.append(lax.dot_general(moved, window, NT, preferred_element_type=F32))
    total = jnp.where(same, total_of(terms), 0.0)
    summed = jnp.sum(total.reshape(TAPS, GROUP, span), axis=1)
    return jnp.concatenate([summed, jnp.zeros((1, span), F32)], axis=0)


def inner_kernel(
    x_ref, g_ref, kernel_ref, vec_ref, bin_ref, win_ref, wint_ref, wout_ref, woutt_ref,
    taps_ref, back_ref, out_ref, gz_ref, dwin_ref, dwout_ref, dtaps_ref,
    *kept,
):
    hidden_units = win_ref.shape[1]
    spread_taps(kernel_ref, taps_ref, False)
    spread_taps(kernel_ref, back_ref, True)
    weights = (vec_ref, bin_ref, win_ref, wint_ref, wout_ref, woutt_ref)
    all_rows(x_ref, g_ref.at[pl.ds(REACH, out_ref.shape[0])], taps_ref, weights, out_ref, gz_ref, kept)
    for start in range(0, hidden_units, 256):
        for index, ref in enumerate((dwin_ref, dwout_ref)):
            ref[:, start : start + 256] = weight_terms(kept, start, 256, index)
    for group in range(x_ref.shape[1] // GROUP):
        dtaps_ref[group] = tap_terms(x_ref, gz_ref, group)


def upper_kernel(
    x_ref, above_ref, g_ref, taps_ref, vec_ref, bin_ref, win_ref, wint_ref, wout_ref, woutt_ref,
    dwin_in_ref, dwout_in_ref, dtaps_in_ref,
    out_ref, gz_ref, dwin_ref, dwout_ref, dtaps_ref,
    tall_ref, *kept,
):
    hidden_units = win_ref.shape[1]
    tall_ref[0:REACH] = above_ref[...]
    tall_ref[REACH:] = x_ref[0 : 2 * REACH]
    weights = (vec_ref, bin_ref, win_ref, wint_ref, wout_ref, woutt_ref)
    all_rows(tall_ref, g_ref.at[pl.ds(0, REACH)], taps_ref, weights, out_ref, gz_ref, kept)
    for start in range(0, hidden_units, 256):
        part = slice(start, start + 256)
        for index, (ref, before_ref) in enumerate(((dwin_ref, dwin_in_ref), (dwout_ref, dwout_in_ref))):
            ref[:, part] = weight_terms(kept, start, 256, index) + before_ref[:, part]
    for group in range(x_ref.shape[1] // GROUP):
        dtaps_ref[group] = tap_terms(tall_ref, gz_ref, group) + dtaps_in_ref[group]


def lower_kernel(
    x_ref, below_ref, g_ref, taps_ref, vec_ref, bin_ref, win_ref, wint_ref, wout_ref, woutt_ref,
    out_ref, gz_ref, tall_ref, *kept,
):
    rows = x_ref.shape[0]
    tall_ref[0 : 2 * REACH] = x_ref[rows - 2 * REACH :]
    tall_ref[2 * REACH :] = below_ref[...]
    weights = (vec_ref, bin_ref, win_ref, wint_ref, wout_ref, woutt_ref)
    all_rows(tall_ref, g_ref.at[pl.ds(rows - REACH, REACH)], taps_ref, weights, out_ref, gz_ref, kept)


def terms_kernel(
    core_ref, tall_ref, gz_ref, normed_ref, act_ref, gout_ref, gh_ref, dwin_ref, dwout_ref, dtaps_ref,
    keep_ref, send_ref, halves_ref, *, scale,
):
    chans, hidden_units = dwin_ref.shape
    kept = (normed_ref, act_ref, gout_ref, gh_ref)
    blocks = hidden_units // 128
    for index, ref in enumerate((dwin_ref, dwout_ref)):
        for start in range(0, hidden_units, 256):
            total = (weight_terms(kept, start, 256, index) + ref[:, start : start + 256]) * scale
            for lanes in range(2):
                block = start // 128 + lanes
                halves_ref[index, block * chans : (block + 1) * chans, :] = total[
                    :, lanes * 128 : (lanes + 1) * 128
                ].astype(BF16)
    at = blocks * chans
    groups = chans // GROUP
    halves_ref[:, at:, :] = jnp.zeros((2, halves_ref.shape[1] - at, 128), BF16)
    span = TAPS * GROUP
    for pair in range(groups // 2):
        both = [
            (tap_terms(tall_ref, gz_ref, group) + dtaps_ref[group]) * scale for group in (2 * pair, 2 * pair + 1)
        ]
        both = jnp.concatenate(both, axis=0)
        both = jnp.concatenate([both, jnp.zeros((16, 128 - span), F32)], axis=1)
        half, place = divmod(pair, groups // 4)
        halves_ref[half, at + place * 16 : at + (place + 1) * 16, :] = both.astype(BF16)
    core = core_ref[0]
    keep_ref[...] = halves_ref[core]
    send_ref[...] = halves_ref[1 - core]


def input_kernel(
    out_upper_ref, out_inner_ref, out_lower_ref, gz_upper_ref, gz_inner_ref, gz_lower_ref,
    below_ref, g_ref, taps_ref,
    out_ref, grad_ref, tall_ref,
):
    rows = g_ref.shape[0]
    at = 0
    for ref in (gz_upper_ref, gz_inner_ref, gz_lower_ref, below_ref):
        tall_ref[at : at + ref.shape[0]] = ref[...]
        at += ref.shape[0]
    at = 0
    for ref in (out_upper_ref, out_inner_ref, out_lower_ref):
        out_ref[at : at + ref.shape[0]] = ref[...]
        at += ref.shape[0]

    def step(row, carry):
        at = row + REACH
        grad_ref[at] = (g_ref[at].astype(F32) + conv_row(tall_ref, taps_ref, row)).astype(BF16)
        return carry

    lax.fori_loop(0, rows - REACH, step, 0)


def input_upper_kernel(
    above_ref, gz_upper_ref, gz_inner_ref, gz_lower_ref, g_ref, taps_ref, rest_ref,
    grad_ref, tall_ref, part_ref, sem,
):
    tall_ref[0:REACH] = above_ref[...]
    tall_ref[REACH : 2 * REACH] = gz_upper_ref[...]
    inner = gz_inner_ref.shape[0]
    for at in range(REACH):
        tall_ref[2 * REACH + at] = gz_inner_ref[at] if at < inner else gz_lower_ref[at - inner]

    def step(row, carry):
        part_ref[row] = (g_ref[row].astype(F32) + conv_row(tall_ref, taps_ref, row)).astype(BF16)
        return carry

    lax.fori_loop(0, REACH, step, 0)
    copy = pltpu.make_async_copy(part_ref, grad_ref.at[pl.ds(0, REACH)], sem)
    copy.start()
    copy.wait()


def final_kernel(place_ref, mine_ref, other_ref, win_ref, woutt_ref, taps_ref, all_ref):
    core, quarter = place_ref[0], place_ref[1]
    chans, hidden_units = win_ref.shape
    size = mine_ref.shape[1]
    for turn in range(4):
        at = pl.ds(pl.multiple_of((quarter ^ turn) * size, 16), size)
        all_ref[core, at, :] = mine_ref[turn]
        all_ref[1 - core, at, :] = other_ref[turn]
    blocks = hidden_units // 128
    for index, ref in enumerate((win_ref, woutt_ref)):
        for block in range(blocks):
            ref[:, block * 128 : (block + 1) * 128] = all_ref[index, block * chans : (block + 1) * chans, :].astype(F32)
    groups = chans // GROUP
    for pair in range(groups // 2):
        half, place = divmod(pair, groups // 4)
        at = blocks * chans + place * 16
        both = all_ref[half, at : at + 16, :].astype(F32)
        for side in range(2):
            group = 2 * pair + side
            piece = both[side * 8 : side * 8 + 8]
            for tap in range(TAPS):
                taps_ref[tap, :, group * GROUP : (group + 1) * GROUP] = piece[:TAPS, tap * GROUP : (tap + 1) * GROUP]


def edge_kernel(x_ref, edge_ref, sem, *, start):
    copy = pltpu.make_async_copy(x_ref.at[pl.ds(start, REACH)], edge_ref, sem)
    copy.start()
    copy.wait()


PARAMS = pltpu.CompilerParams(vmem_limit_bytes=20 * 1024 * 1024)
SMALL = pltpu.CompilerParams(vmem_limit_bytes=4 * 1024 * 1024)
IN_VMEM = pl.BlockSpec(memory_space=pltpu.VMEM)
IN_SMEM = pl.BlockSpec(memory_space=pltpu.SMEM)


def swap(value, axis, mask):
    count = lax.axis_size(axis)
    return lax.ppermute(value, axis, [(source, source ^ mask) for source in range(count)])


def added(*terms):
    terms = [term.astype(F32) for term in terms]
    while len(terms) > 1:
        terms = [terms[at] + terms[at + 1] for at in range(0, len(terms), 2)]
    return terms[0].astype(BF16)


def on_device(
    features, dw_kernel, dw_bias, ln_gain, ln_bias, w_in, b_in, w_out, b_out, layer_scale, cotangent
):
    core = lax.axis_index("core").astype(jnp.uint32)
    quarter = (2 * lax.axis_index("x") + lax.axis_index("space") % 2).astype(jnp.uint32)
    turns = [quarter ^ turn for turn in range(4)]
    place = jnp.stack([core, quarter]).astype(jnp.int32)
    features, place, *turns = lax.optimization_barrier((features, place, *turns))
    x = jnp.swapaxes(features[0, 0], 1, 2)
    g = jnp.swapaxes(cotangent[0, 0], 1, 2)
    rows, chans, width = x.shape
    hidden_units = w_in.shape[1]
    strips = lax.axis_size("space")
    narrow = jax.ShapeDtypeStruct((REACH, chans, width), BF16)
    image = jax.ShapeDtypeStruct((rows, chans, width), BF16)

    def edge(start):
        return pl.pallas_call(
            lambda *refs: edge_kernel(*refs, start=start),
            out_shape=narrow,
            in_specs=[pl.BlockSpec(memory_space=pl.ANY)],
            out_specs=IN_VMEM,
            scratch_shapes=[pltpu.SemaphoreType.DMA(())],
            compiler_params=SMALL,
        )(x)

    above = shifted(edge(rows - REACH), "space", 1)
    vectors = jnp.stack([dw_bias, ln_gain, ln_bias, b_out, layer_scale], axis=1)
    weights = (vectors, b_in[:, None], w_in, w_in.T, w_out, w_out.T)
    devices = lax.axis_size("x") * lax.axis_size("core") * strips
    scale = float(devices * rows * width) ** (-0.5)
    groups = chans // GROUP
    span = TAPS * GROUP
    inner = rows - 2 * REACH

    tall = jax.ShapeDtypeStruct((3 * REACH, chans, width), BF16)

    def kept(count):
        small = jax.ShapeDtypeStruct((count, chans, width), BF16)
        large = jax.ShapeDtypeStruct((count, hidden_units, width), BF16)
        return (small, large, small, large)

    def scratch(shapes):
        return [pltpu.VMEM(shape.shape, shape.dtype) for shape in shapes]

    middle = jax.ShapeDtypeStruct((inner, chans, width), BF16)
    spread = jax.ShapeDtypeStruct((groups, span, 2 * span), BF16)
    matrix = jax.ShapeDtypeStruct((chans, hidden_units), F32)
    terms = (matrix, matrix, jax.ShapeDtypeStruct((groups, 8, span), F32))
    taps, back_taps, out_inner, gz_inner, *inner_terms = pl.pallas_call(
        inner_kernel,
        out_shape=(spread, spread, middle, middle, *terms),
        in_specs=[IN_VMEM] * 9,
        out_specs=(IN_VMEM,) * 7,
        scratch_shapes=scratch(kept(inner)),
        compiler_params=PARAMS,
    )(x, g, dw_kernel, *weights)
    above, top, out_inner = lax.optimization_barrier((above, edge(0), out_inner))
    below = shifted(top, "space", -1)
    half_rows = hidden_units // 128 * chans + groups // 2 * 8
    half_rows = (half_rows + 63) // 64 * 64
    half = jax.ShapeDtypeStruct((half_rows, 128), BF16)
    out_upper, gz_upper, *upper_terms = pl.pallas_call(
        upper_kernel,
        out_shape=(narrow, narrow, *terms),
        in_specs=[IN_VMEM] * 13,
        out_specs=(IN_VMEM,) * 5,
        scratch_shapes=scratch((tall, *kept(REACH))),
        compiler_params=PARAMS,
    )(x, above, g, taps, *weights, *inner_terms)
    gz_below = shifted(gz_upper, "space", -1)
    out_lower, gz_lower, *lower_kept = pl.pallas_call(
        lower_kernel,
        out_shape=(narrow, narrow, tall, *kept(REACH)),
        in_specs=[IN_VMEM] * 10,
        out_specs=(IN_VMEM,) * 7,
        compiler_params=PARAMS,
    )(x, below, g, taps, *weights)
    gz_above = shifted(gz_lower, "space", 1)
    keep, send = pl.pallas_call(
        lambda *refs: terms_kernel(*refs, scale=scale),
        out_shape=(half, half),
        in_specs=[IN_SMEM] + [IN_VMEM] * 9,
        out_specs=(IN_VMEM,) * 2,
        scratch_shapes=[pltpu.VMEM((2, half_rows, 128), BF16)],
        compiler_params=PARAMS,
    )(place, lower_kept[0], gz_lower, *lower_kept[1:], *upper_terms)
    keep, send, gz_below = lax.optimization_barrier((keep, send, gz_below))

    summed = added(keep, swap(send, "core", 1)).reshape(4, half_rows // 4, 128)

    def at(turn):
        return lax.dynamic_index_in_dim(summed, turns[turn], 0, keepdims=False)

    def partner(value, turn):
        return swap(value, ("x", "space"), (turn >> 1) * strips | (turn & 1))

    own = added(at(0), *[partner(at(turn), turn) for turn in (1, 2, 3)])
    out, grad_rest = pl.pallas_call(
        input_kernel,
        out_shape=(image, image),
        in_specs=[IN_VMEM] * 9,
        out_specs=(IN_VMEM, IN_VMEM),
        scratch_shapes=[pltpu.VMEM((rows + REACH, chans, width), BF16)],
        compiler_params=PARAMS,
    )(out_upper, out_inner, out_lower, gz_upper, gz_inner, gz_lower, gz_below, g, back_taps)
    own, grad_rest = lax.optimization_barrier((own, grad_rest))
    bit = 2
    while bit < strips:
        masks = (bit, 2 * bit, 3 * bit) if 2 * bit < strips else (bit,)
        own = added(own, *[swap(own, "space", mask) for mask in masks])
        bit *= 4
    mine = jnp.stack([own] + [partner(own, turn) for turn in (1, 2, 3)])
    grad_input = pl.pallas_call(
        input_upper_kernel,
        out_shape=image,
        in_specs=[IN_VMEM] * 6 + [pl.BlockSpec(memory_space=pl.ANY)],
        out_specs=pl.BlockSpec(memory_space=pl.ANY),
        scratch_shapes=[
            pltpu.VMEM((3 * REACH, chans, width), BF16),
            pltpu.VMEM((REACH, chans, width), BF16),
            pltpu.SemaphoreType.DMA(()),
        ],
        input_output_aliases={6: 0},
        compiler_params=PARAMS,
    )(gz_above, gz_upper, gz_inner, gz_lower, g, back_taps, grad_rest)
    mine, grad_input = lax.optimization_barrier((mine, grad_input))
    other = swap(mine, "core", 1)
    grad_w_in, grad_w_out_t, grad_kernel = pl.pallas_call(
        final_kernel,
        out_shape=(matrix, matrix, jax.ShapeDtypeStruct((TAPS, TAPS, chans), F32)),
        in_specs=[IN_SMEM, IN_VMEM, IN_VMEM],
        out_specs=(IN_VMEM,) * 3,
        scratch_shapes=[pltpu.VMEM((2, half_rows, 128), BF16)],
        compiler_params=PARAMS,
    )(place, mine, other)
    block_output = jnp.swapaxes(out, 1, 2)[None, None]
    grad_image = jnp.swapaxes(grad_input, 1, 2)[None, None]
    return (block_output, grad_image, grad_w_in, grad_w_out_t.T, grad_kernel)


def solution(mesh):
    slides, strips = mesh.devices.shape
    split = Mesh(mesh.devices.reshape(slides // 2, 2, strips), ("x", "core", "space"))
    placed = P(("x", "core"), "space", None, None, None)
    return jax.shard_map(
        on_device,
        mesh=split,
        in_specs=(placed,) + (P(),) * 9 + (placed,),
        out_specs=(placed, placed, P(), P(), P()),
        check_vma=False,
    )
```

```python
import jax
import jax.numpy as jnp
from jax import lax
from jax.experimental import pallas as pl
from jax.experimental.pallas import tpu as pltpu
from jax.sharding import Mesh
from jax.sharding import PartitionSpec as P

EPSILON = 1e-06
TAPS = 7
REACH = 3
GROUP = 16
BF16 = jnp.bfloat16
F32 = jnp.float32


def slide_lanes(value, steps):
    if steps == 0:
        return value
    width = value.shape[-1]
    lane = lax.broadcasted_iota(jnp.int32, value.shape, value.ndim - 1)
    moved = pltpu.roll(value, (-steps) % width, value.ndim - 1)
    keep = lane < width - steps if steps > 0 else lane >= -steps
    return jnp.where(keep, moved, jnp.zeros_like(moved))


def conv_row(tall_ref, taps_ref, row):
    _, chans, width = tall_ref.shape
    pieces = []
    for group in range(chans // GROUP):
        window = tall_ref[pl.ds(row, TAPS), group * GROUP : (group + 1) * GROUP, :]
        window = window.reshape(TAPS * GROUP, width)
        window = jnp.concatenate([window, window], axis=0)
        parts = jnp.dot(taps_ref[group], window, preferred_element_type=F32)
        total = None
        for tap in range(TAPS):
            part = slide_lanes(parts[tap * GROUP : (tap + 1) * GROUP], tap - REACH)
            total = part if total is None else total + part
        pieces.append(total)
    return jnp.concatenate(pieces, axis=0)


def spread_taps(kernel_ref, taps_ref, flipped):
    chans = kernel_ref.shape[2]
    span = TAPS * GROUP
    same = lax.broadcasted_iota(jnp.int32, (GROUP, span), 0) == lax.broadcasted_iota(
        jnp.int32, (GROUP, span), 1
    ) % GROUP
    for group in range(chans // GROUP):
        lanes = slice(group * GROUP, (group + 1) * GROUP)
        order = [TAPS - 1 - tap if flipped else tap for tap in range(TAPS)]
        across = jnp.concatenate([kernel_ref[tap, :, lanes] for tap in order], axis=1)
        for tap in range(TAPS):
            source = TAPS - 1 - tap if flipped else tap
            wide = jnp.broadcast_to(across[source : source + 1], (GROUP, span))
            wide = jnp.where(same, wide, 0.0)
            high = wide.astype(BF16)
            low = (wide - high.astype(F32)).astype(BF16)
            taps_ref[group, tap * GROUP : (tap + 1) * GROUP, :] = jnp.concatenate([high, low], axis=1)


def one_row(row, tall_ref, g_ref, taps_ref, weights, out_ref, gz_ref, kept):
    vec_ref, bin_ref, win_ref, wint_ref, wout_ref, woutt_ref = weights
    normed_ref, act_ref, gout_ref, gh_ref = kept

    width = g_ref.shape[2]

    def vec(index):
        return across(vec_ref[index], width)

    hidden_units = win_ref.shape[1]
    mixed = conv_row(tall_ref, taps_ref, row) + vec(0)
    centre = mixed - jnp.mean(mixed, axis=0, keepdims=True)
    inverse = lax.rsqrt(jnp.mean(centre * centre, axis=0, keepdims=True) + EPSILON)
    unit = centre * inverse
    normed = (unit * vec(1) + vec(2)).astype(BF16)
    normed_ref[row] = normed
    gout = (vec(4) * g_ref[row].astype(F32)).astype(BF16)
    gout_ref[row] = gout
    span = 256
    for start in range(0, hidden_units, span):
        part = slice(start, start + span)
        hidden = jnp.dot(wint_ref[part, :], normed, preferred_element_type=F32) + across(bin_ref[part, :], width)
        grad_act = jnp.dot(wout_ref[part, :], gout, preferred_element_type=F32)
        cdf = 0.5 * (1.0 + lax.erf(hidden * 0.7071067811865476))
        slope = cdf + hidden * jnp.exp(-0.5 * hidden * hidden) * 0.3989422804014327
        act_ref[row, part, :] = (hidden * cdf).astype(BF16)
        gh_ref[row, part, :] = (grad_act * slope).astype(BF16)
    branch = jnp.dot(woutt_ref[...], act_ref[row], preferred_element_type=F32) + vec(3)
    out_ref[row] = (tall_ref[row + REACH].astype(F32) + vec(4) * branch).astype(BF16)
    grad_norm = jnp.dot(win_ref[...], gh_ref[row], preferred_element_type=F32) * vec(1)
    grad_mixed = inverse * (
        grad_norm
        - jnp.mean(grad_norm, axis=0, keepdims=True)
        - unit * jnp.mean(grad_norm * unit, axis=0, keepdims=True)
    )
    gz_ref[row] = grad_mixed.astype(BF16)


def all_rows(tall_ref, g_ref, taps_ref, weights, out_ref, gz_ref, kept):
    def step(row, carry):
        one_row(row, tall_ref, g_ref, taps_ref, weights, out_ref, gz_ref, kept)
        return carry

    lax.fori_loop(0, out_ref.shape[0], step, 0)


NT = (((1,), (1,)), ((), ()))


def total_of(terms):
    total = terms[0]
    for term in terms[1:]:
        total = total + term
    return total


def weight_terms(kept, start, width, index):
    normed_ref, act_ref, gout_ref, gh_ref = kept
    left, right = ((normed_ref, gh_ref), (gout_ref, act_ref))[index]
    return total_of(
        [
            lax.dot_general(left[row], right[row, start : start + width, :], NT, preferred_element_type=F32)
            for row in range(left.shape[0])
        ]
    )


def tap_terms(tall_ref, gz_ref, group):
    span = TAPS * GROUP
    same = lax.broadcasted_iota(jnp.int32, (span, span), 0) % GROUP == lax.broadcasted_iota(
        jnp.int32, (span, span), 1
    ) % GROUP
    lanes = slice(group * GROUP, (group + 1) * GROUP)
    terms = []
    for row in range(gz_ref.shape[0]):
        grad = gz_ref[row, lanes, :].astype(F32)
        moved = jnp.concatenate([slide_lanes(grad, REACH - tap) for tap in range(TAPS)], axis=0).astype(BF16)
        window = tall_ref[row : row + TAPS, lanes, :].reshape(span, -1)
        terms.append(lax.dot_general(moved, window, NT, preferred_element_type=F32))
    total = jnp.where(same, total_of(terms), 0.0)
    summed = jnp.sum(total.reshape(TAPS, GROUP, span), axis=1)
    return jnp.concatenate([summed, jnp.zeros((1, span), F32)], axis=0)


def prepare_kernel(
    kernel_ref, win_ref, woutt_ref, bin_in_ref, *refs
):
    count = len(refs) - 6
    vectors, (taps_ref, back_ref, vec_ref, bin_ref, wint_ref, wout_ref) = refs[:count], refs[count:]
    spread_taps(kernel_ref, taps_ref, False)
    spread_taps(kernel_ref, back_ref, True)
    for source, target in ((win_ref, wint_ref), (woutt_ref, wout_ref)):
        target[...] = source[...].T
    chans = vec_ref.shape[1]
    for index, ref in enumerate(vectors):
        row = jnp.concatenate([ref[...], jnp.zeros((1, -chans % 128), F32)], axis=1)
        for start in range(0, chans, 128):
            size = min(128, chans - start)
            square = jnp.broadcast_to(row[:, start : start + 128], (128, 128)).T
            vec_ref[index, start : start + size, :] = square[:size]
    for index in range(bin_in_ref.shape[0]):
        square = jnp.broadcast_to(bin_in_ref[index : index + 1, :], (128, 128))
        bin_ref[index * 128 : (index + 1) * 128, :] = square.T


def across(value, width):
    return jnp.concatenate([value] * (width // 128), axis=1)


def inner_kernel(
    x_ref, g_ref, taps_ref, vec_ref, bin_ref, win_ref, wint_ref, wout_ref, woutt_ref,
    out_ref, gz_ref, dwin_ref, dwout_ref, dtaps_ref,
    *kept,
):
    hidden_units = win_ref.shape[1]
    weights = (vec_ref, bin_ref, win_ref, wint_ref, wout_ref, woutt_ref)
    all_rows(x_ref, g_ref.at[pl.ds(REACH, out_ref.shape[0])], taps_ref, weights, out_ref, gz_ref, kept)
    for start in range(0, hidden_units, 256):
        for index, ref in enumerate((dwin_ref, dwout_ref)):
            ref[:, start : start + 256] = weight_terms(kept, start, 256, index)
    for group in range(x_ref.shape[1] // GROUP):
        dtaps_ref[group] = tap_terms(x_ref, gz_ref, group)


def with_halo(x_ref, halo_ref, tall_ref, low):
    shared = 2 * REACH
    tall_ref[pl.ds(shared * low, REACH)] = halo_ref[...]
    tall_ref[pl.ds(REACH * (1 - low), shared)] = x_ref[pl.ds((x_ref.shape[0] - shared) * low, shared)]


def first_kernel(
    place_ref, x_ref, halo_ref, g_ref, taps_ref, vec_ref, bin_ref, win_ref, wint_ref, wout_ref, woutt_ref,
    dwin_in_ref, dwout_in_ref, dtaps_in_ref,
    out_ref, gz_ref, dwin_ref, dwout_ref, dtaps_ref,
    tall_ref, *kept,
):
    hidden_units = win_ref.shape[1]
    low = place_ref[2]
    with_halo(x_ref, halo_ref, tall_ref, low)
    weights = (vec_ref, bin_ref, win_ref, wint_ref, wout_ref, woutt_ref)
    rows = g_ref.at[pl.ds((x_ref.shape[0] - REACH) * low, REACH)]
    all_rows(tall_ref, rows, taps_ref, weights, out_ref, gz_ref, kept)
    for start in range(0, hidden_units, 256):
        part = slice(start, start + 256)
        for index, (ref, before_ref) in enumerate(((dwin_ref, dwin_in_ref), (dwout_ref, dwout_in_ref))):
            ref[:, part] = weight_terms(kept, start, 256, index) + before_ref[:, part]
    for group in range(x_ref.shape[1] // GROUP):
        dtaps_ref[group] = tap_terms(tall_ref, gz_ref, group) + dtaps_in_ref[group]


def second_kernel(
    place_ref, x_ref, halo_ref, g_ref, taps_ref, vec_ref, bin_ref, win_ref, wint_ref, wout_ref, woutt_ref,
    out_ref, gz_ref, tall_ref, *kept,
):
    low = 1 - place_ref[2]
    with_halo(x_ref, halo_ref, tall_ref, low)
    weights = (vec_ref, bin_ref, win_ref, wint_ref, wout_ref, woutt_ref)
    rows = g_ref.at[pl.ds((x_ref.shape[0] - REACH) * low, REACH)]
    all_rows(tall_ref, rows, taps_ref, weights, out_ref, gz_ref, kept)


def terms_kernel(
    core_ref, tall_ref, gz_ref, normed_ref, act_ref, gout_ref, gh_ref, dwin_ref, dwout_ref, dtaps_ref,
    keep_ref, send_ref, halves_ref, *, scale,
):
    chans, hidden_units = dwin_ref.shape
    kept = (normed_ref, act_ref, gout_ref, gh_ref)
    blocks = hidden_units // 128
    for index, ref in enumerate((dwin_ref, dwout_ref)):
        for start in range(0, hidden_units, 256):
            total = (weight_terms(kept, start, 256, index) + ref[:, start : start + 256]) * scale
            for lanes in range(2):
                block = start // 128 + lanes
                halves_ref[index, block * chans : (block + 1) * chans, :] = total[
                    :, lanes * 128 : (lanes + 1) * 128
                ].astype(BF16)
    at = blocks * chans
    groups = chans // GROUP
    halves_ref[:, at:, :] = jnp.zeros((2, halves_ref.shape[1] - at, 128), BF16)
    span = TAPS * GROUP
    for pair in range(groups // 2):
        both = [
            (tap_terms(tall_ref, gz_ref, group) + dtaps_ref[group]) * scale for group in (2 * pair, 2 * pair + 1)
        ]
        both = jnp.concatenate(both, axis=0)
        both = jnp.concatenate([both, jnp.zeros((16, 128 - span), F32)], axis=1)
        half, place = divmod(pair, groups // 4)
        halves_ref[half, at + place * 16 : at + (place + 1) * 16, :] = both.astype(BF16)
    core = core_ref[0]
    keep_ref[...] = halves_ref[core]
    send_ref[...] = halves_ref[1 - core]


def input_kernel(
    place_ref, out_first_ref, out_inner_ref, out_second_ref, gz_first_ref, gz_inner_ref, gz_second_ref,
    halo_ref, g_ref, taps_ref,
    out_ref, grad_ref, tall_ref,
):
    low = place_ref[2]
    rows = g_ref.shape[0]
    inner = rows - 2 * REACH
    tall_ref[pl.ds(rows * (1 - low), REACH)] = gz_second_ref[...]
    tall_ref[pl.ds(REACH * (2 - low), inner)] = gz_inner_ref[...]
    tall_ref[pl.ds(REACH + inner * low, REACH)] = gz_first_ref[...]
    tall_ref[pl.ds(rows * low, REACH)] = halo_ref[...]
    out_ref[REACH : REACH + inner] = out_inner_ref[...]
    out_ref[pl.ds((rows - REACH) * low, REACH)] = out_first_ref[...]
    out_ref[pl.ds((rows - REACH) * (1 - low), REACH)] = out_second_ref[...]

    def step(row, carry):
        at = row + REACH * low
        grad_ref[at] = (g_ref[at].astype(F32) + conv_row(tall_ref, taps_ref, row)).astype(BF16)
        return carry

    lax.fori_loop(0, rows - REACH, step, 0)


def input_rest_kernel(
    place_ref, halo_ref, gz_first_ref, gz_inner_ref, gz_second_ref, g_ref, taps_ref, rest_ref,
    grad_ref, tall_ref, part_ref, sem,
):
    low = 1 - place_ref[2]
    rows = g_ref.shape[0]
    inner = rows - 2 * REACH
    near = REACH - inner
    tall_ref[pl.ds(2 * REACH * low, REACH)] = halo_ref[...]
    tall_ref[REACH : 2 * REACH] = gz_second_ref[...]
    tall_ref[pl.ds(2 * REACH * (1 - low) + near * low, inner)] = gz_inner_ref[...]
    tall_ref[pl.ds((2 * REACH + inner) * (1 - low), near)] = gz_first_ref[pl.ds((REACH - near) * low, near)]
    first = (rows - REACH) * low

    def step(row, carry):
        part_ref[row] = (g_ref[first + row].astype(F32) + conv_row(tall_ref, taps_ref, row)).astype(BF16)
        return carry

    lax.fori_loop(0, REACH, step, 0)
    copy = pltpu.make_async_copy(part_ref, grad_ref.at[pl.ds(first, REACH)], sem)
    copy.start()
    copy.wait()


def final_kernel(place_ref, mine_ref, other_ref, win_ref, woutt_ref, taps_ref, all_ref):
    core, quarter = place_ref[0], place_ref[1]
    chans, hidden_units = win_ref.shape
    size = mine_ref.shape[1]
    for turn in range(4):
        at = pl.ds(pl.multiple_of((quarter ^ turn) * size, 16), size)
        all_ref[core, at, :] = mine_ref[turn]
        all_ref[1 - core, at, :] = other_ref[turn]
    blocks = hidden_units // 128
    for index, ref in enumerate((win_ref, woutt_ref)):
        for block in range(blocks):
            ref[:, block * 128 : (block + 1) * 128] = all_ref[index, block * chans : (block + 1) * chans, :].astype(F32)
    groups = chans // GROUP
    for pair in range(groups // 2):
        half, place = divmod(pair, groups // 4)
        at = blocks * chans + place * 16
        both = all_ref[half, at : at + 16, :].astype(F32)
        for side in range(2):
            group = 2 * pair + side
            piece = both[side * 8 : side * 8 + 8]
            for tap in range(TAPS):
                taps_ref[tap, :, group * GROUP : (group + 1) * GROUP] = piece[:TAPS, tap * GROUP : (tap + 1) * GROUP]


def edge_kernel(place_ref, x_ref, edge_ref, *, first):
    low = place_ref[2] if first else 1 - place_ref[2]
    edge_ref[...] = x_ref[pl.ds((x_ref.shape[0] - REACH) * low, REACH)]


PARAMS = pltpu.CompilerParams(vmem_limit_bytes=20 * 1024 * 1024)
SMALL = pltpu.CompilerParams(vmem_limit_bytes=8 * 1024 * 1024)
IN_VMEM = pl.BlockSpec(memory_space=pltpu.VMEM)
IN_SMEM = pl.BlockSpec(memory_space=pltpu.SMEM)


def swap(value, axis, mask):
    count = lax.axis_size(axis)
    return lax.ppermute(value, axis, [(source, source ^ mask) for source in range(count)])


def added(*terms):
    terms = [term.astype(F32) for term in terms]
    while len(terms) > 1:
        terms = [terms[at] + terms[at + 1] for at in range(0, len(terms), 2)]
    return terms[0].astype(BF16)


def on_device(
    features, dw_kernel, dw_bias, ln_gain, ln_bias, w_in, b_in, w_out, b_out, layer_scale, cotangent
):
    core = lax.axis_index("core").astype(jnp.uint32)
    quarter = (2 * lax.axis_index("x") + lax.axis_index("space") % 2).astype(jnp.uint32)
    turns = [quarter ^ turn for turn in range(4)]
    even = (1 - lax.axis_index("space") % 2).astype(jnp.uint32)
    place = jnp.stack([core, quarter, even]).astype(jnp.int32)
    features, place, *turns = lax.optimization_barrier((features, place, *turns))
    x = jnp.swapaxes(features[0, 0], 1, 2)
    g = jnp.swapaxes(cotangent[0, 0], 1, 2)
    rows, chans, width = x.shape
    hidden_units = w_in.shape[1]
    strips = lax.axis_size("space")
    narrow = jax.ShapeDtypeStruct((REACH, chans, width), BF16)
    image = jax.ShapeDtypeStruct((rows, chans, width), BF16)

    def edge(first):
        return pl.pallas_call(
            lambda *refs: edge_kernel(*refs, first=first),
            out_shape=narrow,
            in_specs=[IN_SMEM, IN_VMEM],
            out_specs=IN_VMEM,
            compiler_params=SMALL,
        )(place, x)

    def first_swap(value):
        return swap(value, "space", 1)

    def second_swap(value):
        pairs = [(low, low + 1) for low in range(1, strips - 1, 2)]
        return lax.ppermute(value, "space", pairs + [(high, low) for low, high in pairs])

    first_halo = first_swap(edge(True))
    devices = lax.axis_size("x") * lax.axis_size("core") * strips
    scale = float(devices * rows * width) ** (-0.5)
    groups = chans // GROUP
    span = TAPS * GROUP
    inner = rows - 2 * REACH

    tall = jax.ShapeDtypeStruct((3 * REACH, chans, width), BF16)

    def kept(count):
        small = jax.ShapeDtypeStruct((count, chans, width), BF16)
        large = jax.ShapeDtypeStruct((count, hidden_units, width), BF16)
        return (small, large, small, large)

    def scratch(shapes):
        return [pltpu.VMEM(shape.shape, shape.dtype) for shape in shapes]

    middle = jax.ShapeDtypeStruct((inner, chans, width), BF16)
    spread = jax.ShapeDtypeStruct((groups, span, 2 * span), BF16)
    matrix = jax.ShapeDtypeStruct((chans, hidden_units), F32)
    terms = (matrix, matrix, jax.ShapeDtypeStruct((groups, 8, span), F32))
    vectors = (dw_bias, ln_gain, ln_bias, b_out, layer_scale)
    across_lanes = jax.ShapeDtypeStruct((len(vectors), chans, 128), F32)
    hidden_lanes = jax.ShapeDtypeStruct((hidden_units, 128), F32)
    turned = jax.ShapeDtypeStruct((hidden_units, chans), BF16)
    taps, back_taps, vectors, bias, w_in_t, w_out_turned = pl.pallas_call(
        prepare_kernel,
        out_shape=(spread, spread, across_lanes, hidden_lanes, turned, turned),
        in_specs=[IN_VMEM] * (4 + len(vectors)),
        out_specs=(IN_VMEM,) * 6,
        compiler_params=SMALL,
    )(dw_kernel, w_in, w_out.T, b_in.reshape(-1, 128), *[vector[None] for vector in vectors])
    weights = (vectors, bias, w_in, w_in_t, w_out_turned, w_out.T)
    second_edge, taps = lax.optimization_barrier((edge(False), taps))
    second_halo = second_swap(second_edge)
    out_inner, gz_inner, *inner_terms = pl.pallas_call(
        inner_kernel,
        out_shape=(middle, middle, *terms),
        in_specs=[IN_VMEM] * 9,
        out_specs=(IN_VMEM,) * 5,
        scratch_shapes=scratch(kept(inner)),
        compiler_params=PARAMS,
    )(x, g, taps, *weights)
    half_rows = hidden_units // 128 * chans + groups // 2 * 8
    half_rows = (half_rows + 63) // 64 * 64
    half = jax.ShapeDtypeStruct((half_rows, 128), BF16)
    out_first, gz_first, *first_terms = pl.pallas_call(
        first_kernel,
        out_shape=(narrow, narrow, *terms),
        in_specs=[IN_SMEM] + [IN_VMEM] * 13,
        out_specs=(IN_VMEM,) * 5,
        scratch_shapes=scratch((tall, *kept(REACH))),
        compiler_params=PARAMS,
    )(place, x, first_halo, g, taps, *weights, *inner_terms)
    gz_first_halo = first_swap(gz_first)
    out_second, gz_second, *second_kept = pl.pallas_call(
        second_kernel,
        out_shape=(narrow, narrow, tall, *kept(REACH)),
        in_specs=[IN_SMEM] + [IN_VMEM] * 10,
        out_specs=(IN_VMEM,) * 7,
        compiler_params=PARAMS,
    )(place, x, second_halo, g, taps, *weights)
    gz_second_halo = second_swap(gz_second)
    keep, send = pl.pallas_call(
        lambda *refs: terms_kernel(*refs, scale=scale),
        out_shape=(half, half),
        in_specs=[IN_SMEM] + [IN_VMEM] * 9,
        out_specs=(IN_VMEM,) * 2,
        scratch_shapes=[pltpu.VMEM((2, half_rows, 128), BF16)],
        compiler_params=PARAMS,
    )(place, second_kept[0], gz_second, *second_kept[1:], *first_terms)
    keep, send, gz_first_halo = lax.optimization_barrier((keep, send, gz_first_halo))

    summed = added(keep, swap(send, "core", 1)).reshape(4, half_rows // 4, 128)

    def at(turn):
        return lax.dynamic_index_in_dim(summed, turns[turn], 0, keepdims=False)

    def partner(value, turn):
        return swap(value, ("x", "space"), (turn >> 1) * strips | (turn & 1))

    own = added(at(0), *[partner(at(turn), turn) for turn in (1, 2, 3)])
    out, grad_rest = pl.pallas_call(
        input_kernel,
        out_shape=(image, image),
        in_specs=[IN_SMEM] + [IN_VMEM] * 9,
        out_specs=(IN_VMEM, IN_VMEM),
        scratch_shapes=[pltpu.VMEM((rows + REACH, chans, width), BF16)],
        compiler_params=PARAMS,
    )(place, out_first, out_inner, out_second, gz_first, gz_inner, gz_second, gz_first_halo, g, back_taps)
    bit = 2
    while bit < strips:
        masks = (bit, 2 * bit, 3 * bit) if 2 * bit < strips else (bit,)
        own = added(own, *[swap(own, "space", mask) for mask in masks])
        bit *= 4
    own, grad_rest = lax.optimization_barrier((own, grad_rest))
    mine = jnp.stack([own] + [partner(own, turn) for turn in (1, 2, 3)])
    grad_input = pl.pallas_call(
        input_rest_kernel,
        out_shape=image,
        in_specs=[IN_SMEM] + [IN_VMEM] * 6 + [pl.BlockSpec(memory_space=pl.ANY)],
        out_specs=pl.BlockSpec(memory_space=pl.ANY),
        scratch_shapes=[
            pltpu.VMEM((3 * REACH, chans, width), BF16),
            pltpu.VMEM((REACH, chans, width), BF16),
            pltpu.SemaphoreType.DMA(()),
        ],
        input_output_aliases={7: 0},
        compiler_params=PARAMS,
    )(place, gz_second_halo, gz_first, gz_inner, gz_second, g, back_taps, grad_rest)
    mine, grad_input = lax.optimization_barrier((mine, grad_input))
    other = swap(mine, "core", 1)
    grad_w_in, grad_w_out_t, grad_kernel = pl.pallas_call(
        final_kernel,
        out_shape=(matrix, matrix, jax.ShapeDtypeStruct((TAPS, TAPS, chans), F32)),
        in_specs=[IN_SMEM, IN_VMEM, IN_VMEM],
        out_specs=(IN_VMEM,) * 3,
        scratch_shapes=[pltpu.VMEM((2, half_rows, 128), BF16)],
        compiler_params=PARAMS,
    )(place, mine, other)
    block_output = jnp.swapaxes(out, 1, 2)[None, None]
    grad_image = jnp.swapaxes(grad_input, 1, 2)[None, None]
    return (block_output, grad_image, grad_w_in, grad_w_out_t.T, grad_kernel)


def solution(mesh):
    slides, strips = mesh.devices.shape
    split = Mesh(mesh.devices.reshape(slides // 2, 2, strips), ("x", "core", "space"))
    placed = P(("x", "core"), "space", None, None, None)
    return jax.shard_map(
        on_device,
        mesh=split,
        in_specs=(placed,) + (P(),) * 9 + (placed,),
        out_specs=(placed, placed, P(), P(), P()),
        check_vma=False,
    )
```

```python
import jax
import jax.numpy as jnp
from jax import lax
from jax.experimental import pallas as pl
from jax.experimental.pallas import tpu as pltpu
from jax.sharding import Mesh
from jax.sharding import PartitionSpec as P

EPSILON = 1e-06
TAPS = 7
REACH = 3
GROUP = 16
BF16 = jnp.bfloat16
F32 = jnp.float32


def slide_lanes(value, steps):
    if steps == 0:
        return value
    width = value.shape[-1]
    lane = lax.broadcasted_iota(jnp.int32, value.shape, value.ndim - 1)
    moved = pltpu.roll(value, (-steps) % width, value.ndim - 1)
    keep = lane < width - steps if steps > 0 else lane >= -steps
    return jnp.where(keep, moved, jnp.zeros_like(moved))


def conv_row(tall_ref, taps_ref, row):
    _, chans, width = tall_ref.shape
    pieces = []
    for group in range(chans // GROUP):
        window = tall_ref[pl.ds(row, TAPS), group * GROUP : (group + 1) * GROUP, :]
        window = window.reshape(TAPS * GROUP, width)
        window = jnp.concatenate([window, window], axis=0)
        parts = jnp.dot(taps_ref[group], window, preferred_element_type=F32)
        total = None
        for tap in range(TAPS):
            part = slide_lanes(parts[tap * GROUP : (tap + 1) * GROUP], tap - REACH)
            total = part if total is None else total + part
        pieces.append(total)
    return jnp.concatenate(pieces, axis=0)


def is_low():
    return 1 - lax.axis_index("space") % 2


def spread_taps(kernel_ref, taps_ref, flipped):
    chans = kernel_ref.shape[2]
    span = TAPS * GROUP
    same = lax.broadcasted_iota(jnp.int32, (GROUP, span), 0) == lax.broadcasted_iota(
        jnp.int32, (GROUP, span), 1
    ) % GROUP
    for group in range(chans // GROUP):
        lanes = slice(group * GROUP, (group + 1) * GROUP)
        order = [TAPS - 1 - tap if flipped else tap for tap in range(TAPS)]
        across = jnp.concatenate([kernel_ref[tap, :, lanes] for tap in order], axis=1)
        for tap in range(TAPS):
            source = TAPS - 1 - tap if flipped else tap
            wide = jnp.broadcast_to(across[source : source + 1], (GROUP, span))
            wide = jnp.where(same, wide, 0.0)
            high = wide.astype(BF16)
            low = (wide - high.astype(F32)).astype(BF16)
            taps_ref[group, tap * GROUP : (tap + 1) * GROUP, :] = jnp.concatenate([high, low], axis=1)


def one_row(row, tall_ref, g_ref, taps_ref, weights, out_ref, gz_ref, kept):
    vec_ref, bin_ref, win_ref, wint_ref, wout_ref, woutt_ref = weights
    normed_ref, act_ref, gout_ref, gh_ref = kept

    width = g_ref.shape[2]

    def vec(index):
        return across(vec_ref[index], width)

    hidden_units = win_ref.shape[1]
    mixed = conv_row(tall_ref, taps_ref, row) + vec(0)
    centre = mixed - jnp.mean(mixed, axis=0, keepdims=True)
    inverse = lax.rsqrt(jnp.mean(centre * centre, axis=0, keepdims=True) + EPSILON)
    unit = centre * inverse
    normed = (unit * vec(1) + vec(2)).astype(BF16)
    normed_ref[row] = normed
    gout = (vec(4) * g_ref[row].astype(F32)).astype(BF16)
    gout_ref[row] = gout
    span = 256
    for start in range(0, hidden_units, span):
        part = slice(start, start + span)
        hidden = jnp.dot(wint_ref[part, :], normed, preferred_element_type=F32) + across(bin_ref[part, :], width)
        grad_act = jnp.dot(wout_ref[part, :], gout, preferred_element_type=F32)
        cdf = 0.5 * (1.0 + lax.erf(hidden * 0.7071067811865476))
        slope = cdf + hidden * jnp.exp(-0.5 * hidden * hidden) * 0.3989422804014327
        act_ref[row, part, :] = (hidden * cdf).astype(BF16)
        gh_ref[row, part, :] = (grad_act * slope).astype(BF16)
    branch = jnp.dot(woutt_ref[...], act_ref[row], preferred_element_type=F32) + vec(3)
    out_ref[row] = (tall_ref[row + REACH].astype(F32) + vec(4) * branch).astype(BF16)
    grad_norm = jnp.dot(win_ref[...], gh_ref[row], preferred_element_type=F32) * vec(1)
    grad_mixed = inverse * (
        grad_norm
        - jnp.mean(grad_norm, axis=0, keepdims=True)
        - unit * jnp.mean(grad_norm * unit, axis=0, keepdims=True)
    )
    gz_ref[row] = grad_mixed.astype(BF16)


def all_rows(tall_ref, g_ref, taps_ref, weights, out_ref, gz_ref, kept):
    def step(row, carry):
        one_row(row, tall_ref, g_ref, taps_ref, weights, out_ref, gz_ref, kept)
        return carry

    lax.fori_loop(0, out_ref.shape[0], step, 0, unroll=True)


NT = (((1,), (1,)), ((), ()))


def total_of(terms):
    total = terms[0]
    for term in terms[1:]:
        total = total + term
    return total


def weight_terms(kept, start, width, index):
    normed_ref, act_ref, gout_ref, gh_ref = kept
    left, right = ((normed_ref, gh_ref), (gout_ref, act_ref))[index]
    return total_of(
        [
            lax.dot_general(left[row], right[row, start : start + width, :], NT, preferred_element_type=F32)
            for row in range(left.shape[0])
        ]
    )


def tap_terms(tall_ref, gz_ref, group):
    span = TAPS * GROUP
    same = lax.broadcasted_iota(jnp.int32, (span, span), 0) % GROUP == lax.broadcasted_iota(
        jnp.int32, (span, span), 1
    ) % GROUP
    lanes = slice(group * GROUP, (group + 1) * GROUP)
    terms = []
    for row in range(gz_ref.shape[0]):
        grad = gz_ref[row, lanes, :].astype(F32)
        moved = jnp.concatenate([slide_lanes(grad, REACH - tap) for tap in range(TAPS)], axis=0).astype(BF16)
        window = tall_ref[row : row + TAPS, lanes, :].reshape(span, -1)
        terms.append(lax.dot_general(moved, window, NT, preferred_element_type=F32))
    total = jnp.where(same, total_of(terms), 0.0)
    summed = jnp.sum(total.reshape(TAPS, GROUP, span), axis=1)
    return jnp.concatenate([summed, jnp.zeros((1, span), F32)], axis=0)


def prepare_kernel(
    kernel_ref, win_ref, woutt_ref, bin_in_ref, *refs
):
    count = len(refs) - 6
    vectors, (taps_ref, back_ref, vec_ref, bin_ref, wint_ref, wout_ref) = refs[:count], refs[count:]
    spread_taps(kernel_ref, taps_ref, False)
    spread_taps(kernel_ref, back_ref, True)
    for source, target in ((win_ref, wint_ref), (woutt_ref, wout_ref)):
        target[...] = source[...].T
    chans = vec_ref.shape[1]
    for index, ref in enumerate(vectors):
        row = jnp.concatenate([ref[...], jnp.zeros((1, -chans % 128), F32)], axis=1)
        for start in range(0, chans, 128):
            size = min(128, chans - start)
            square = jnp.broadcast_to(row[:, start : start + 128], (128, 128)).T
            vec_ref[index, start : start + size, :] = square[:size]
    for index in range(bin_in_ref.shape[0]):
        square = jnp.broadcast_to(bin_in_ref[index : index + 1, :], (128, 128))
        bin_ref[index * 128 : (index + 1) * 128, :] = square.T


def across(value, width):
    return jnp.concatenate([value] * (width // 128), axis=1)


def inner_kernel(
    x_ref, g_ref, taps_ref, vec_ref, bin_ref, win_ref, wint_ref, wout_ref, woutt_ref,
    out_ref, gz_ref, dwin_ref, dwout_ref, dtaps_ref,
    *kept,
):
    hidden_units = win_ref.shape[1]
    weights = (vec_ref, bin_ref, win_ref, wint_ref, wout_ref, woutt_ref)
    all_rows(x_ref, g_ref.at[pl.ds(REACH, out_ref.shape[0])], taps_ref, weights, out_ref, gz_ref, kept)
    for start in range(0, hidden_units, 256):
        for index, ref in enumerate((dwin_ref, dwout_ref)):
            ref[:, start : start + 256] = weight_terms(kept, start, 256, index)
    for group in range(x_ref.shape[1] // GROUP):
        dtaps_ref[group] = tap_terms(x_ref, gz_ref, group)


def with_halo(x_ref, halo_ref, tall_ref, low):
    shared = 2 * REACH
    tall_ref[pl.ds(shared * low, REACH)] = halo_ref[...]
    tall_ref[pl.ds(REACH * (1 - low), shared)] = x_ref[pl.ds((x_ref.shape[0] - shared) * low, shared)]


def first_kernel(
    x_ref, halo_ref, g_ref, taps_ref, vec_ref, bin_ref, win_ref, wint_ref, wout_ref, woutt_ref,
    dwin_in_ref, dwout_in_ref, dtaps_in_ref,
    out_ref, gz_ref, dwin_ref, dwout_ref, dtaps_ref,
    tall_ref, *kept,
):
    hidden_units = win_ref.shape[1]
    low = is_low()
    with_halo(x_ref, halo_ref, tall_ref, low)
    weights = (vec_ref, bin_ref, win_ref, wint_ref, wout_ref, woutt_ref)
    rows = g_ref.at[pl.ds((x_ref.shape[0] - REACH) * low, REACH)]
    all_rows(tall_ref, rows, taps_ref, weights, out_ref, gz_ref, kept)
    for start in range(0, hidden_units, 256):
        part = slice(start, start + 256)
        for index, (ref, before_ref) in enumerate(((dwin_ref, dwin_in_ref), (dwout_ref, dwout_in_ref))):
            ref[:, part] = weight_terms(kept, start, 256, index) + before_ref[:, part]
    for group in range(x_ref.shape[1] // GROUP):
        dtaps_ref[group] = tap_terms(tall_ref, gz_ref, group) + dtaps_in_ref[group]


def second_kernel(
    x_ref, halo_ref, g_ref, taps_ref, vec_ref, bin_ref, win_ref, wint_ref, wout_ref, woutt_ref,
    out_ref, gz_ref, tall_ref, *kept,
):
    low = 1 - is_low()
    with_halo(x_ref, halo_ref, tall_ref, low)
    weights = (vec_ref, bin_ref, win_ref, wint_ref, wout_ref, woutt_ref)
    rows = g_ref.at[pl.ds((x_ref.shape[0] - REACH) * low, REACH)]
    all_rows(tall_ref, rows, taps_ref, weights, out_ref, gz_ref, kept)


def terms_kernel(
    tall_ref, gz_ref, normed_ref, act_ref, gout_ref, gh_ref, dwin_ref, dwout_ref, dtaps_ref,
    keep_ref, send_ref, halves_ref, *, scale,
):
    chans, hidden_units = dwin_ref.shape
    kept = (normed_ref, act_ref, gout_ref, gh_ref)
    blocks = hidden_units // 128
    for index, ref in enumerate((dwin_ref, dwout_ref)):
        for start in range(0, hidden_units, 256):
            total = (weight_terms(kept, start, 256, index) + ref[:, start : start + 256]) * scale
            for lanes in range(2):
                block = start // 128 + lanes
                halves_ref[index, block * chans : (block + 1) * chans, :] = total[
                    :, lanes * 128 : (lanes + 1) * 128
                ].astype(BF16)
    at = blocks * chans
    groups = chans // GROUP
    halves_ref[:, at:, :] = jnp.zeros((2, halves_ref.shape[1] - at, 128), BF16)
    span = TAPS * GROUP
    for pair in range(groups // 2):
        both = [
            (tap_terms(tall_ref, gz_ref, group) + dtaps_ref[group]) * scale for group in (2 * pair, 2 * pair + 1)
        ]
        both = jnp.concatenate(both, axis=0)
        both = jnp.concatenate([both, jnp.zeros((16, 128 - span), F32)], axis=1)
        half, place = divmod(pair, groups // 4)
        halves_ref[half, at + place * 16 : at + (place + 1) * 16, :] = both.astype(BF16)
    core = lax.axis_index("core")
    keep_ref[...] = halves_ref[core]
    send_ref[...] = halves_ref[1 - core]


def input_kernel(
    out_first_ref, out_inner_ref, out_second_ref, gz_first_ref, gz_inner_ref, gz_second_ref,
    halo_ref, g_ref, taps_ref,
    out_ref, grad_ref, tall_ref,
):
    low = is_low()
    rows = g_ref.shape[0]
    inner = rows - 2 * REACH
    tall_ref[pl.ds(rows * (1 - low), REACH)] = gz_second_ref[...]
    tall_ref[pl.ds(REACH * (2 - low), inner)] = gz_inner_ref[...]
    tall_ref[pl.ds(REACH + inner * low, REACH)] = gz_first_ref[...]
    tall_ref[pl.ds(rows * low, REACH)] = halo_ref[...]
    out_ref[REACH : REACH + inner] = out_inner_ref[...]
    out_ref[pl.ds((rows - REACH) * low, REACH)] = out_first_ref[...]
    out_ref[pl.ds((rows - REACH) * (1 - low), REACH)] = out_second_ref[...]

    def step(row, carry):
        at = row + REACH * low
        grad_ref[at] = (g_ref[at].astype(F32) + conv_row(tall_ref, taps_ref, row)).astype(BF16)
        return carry

    lax.fori_loop(0, rows - REACH, step, 0)


def input_rest_kernel(
    halo_ref, gz_first_ref, gz_inner_ref, gz_second_ref, g_ref, taps_ref, rest_ref,
    grad_ref, tall_ref, part_ref, sem,
):
    low = 1 - is_low()
    rows = g_ref.shape[0]
    inner = rows - 2 * REACH
    near = REACH - inner
    tall_ref[pl.ds(2 * REACH * low, REACH)] = halo_ref[...]
    tall_ref[REACH : 2 * REACH] = gz_second_ref[...]
    tall_ref[pl.ds(2 * REACH * (1 - low) + near * low, inner)] = gz_inner_ref[...]
    tall_ref[pl.ds((2 * REACH + inner) * (1 - low), near)] = gz_first_ref[pl.ds((REACH - near) * low, near)]
    first = (rows - REACH) * low

    def step(row, carry):
        part_ref[row] = (g_ref[first + row].astype(F32) + conv_row(tall_ref, taps_ref, row)).astype(BF16)
        return carry

    lax.fori_loop(0, REACH, step, 0)
    copy = pltpu.make_async_copy(part_ref, grad_ref.at[pl.ds(first, REACH)], sem)
    copy.start()
    copy.wait()


def final_kernel(mine_ref, other_ref, win_ref, woutt_ref, taps_ref, all_ref):
    core = lax.axis_index("core")
    quarter = 2 * lax.axis_index("x") + lax.axis_index("space") % 2
    chans, hidden_units = win_ref.shape
    size = mine_ref.shape[1]
    for turn in range(4):
        at = pl.ds(pl.multiple_of((quarter ^ turn) * size, 16), size)
        all_ref[core, at, :] = mine_ref[turn]
        all_ref[1 - core, at, :] = other_ref[turn]
    blocks = hidden_units // 128
    for index, ref in enumerate((win_ref, woutt_ref)):
        for block in range(blocks):
            ref[:, block * 128 : (block + 1) * 128] = all_ref[index, block * chans : (block + 1) * chans, :].astype(F32)
    groups = chans // GROUP
    for pair in range(groups // 2):
        half, place = divmod(pair, groups // 4)
        at = blocks * chans + place * 16
        both = all_ref[half, at : at + 16, :].astype(F32)
        for side in range(2):
            group = 2 * pair + side
            piece = both[side * 8 : side * 8 + 8]
            for tap in range(TAPS):
                taps_ref[tap, :, group * GROUP : (group + 1) * GROUP] = piece[:TAPS, tap * GROUP : (tap + 1) * GROUP]


def edge_kernel(x_ref, edge_ref, *, first):
    low = is_low() if first else 1 - is_low()
    edge_ref[...] = x_ref[pl.ds((x_ref.shape[0] - REACH) * low, REACH)]


PARAMS = pltpu.CompilerParams(vmem_limit_bytes=20 * 1024 * 1024)
SMALL = pltpu.CompilerParams(vmem_limit_bytes=8 * 1024 * 1024)
IN_VMEM = pl.BlockSpec(memory_space=pltpu.VMEM)


def swap(value, axis, mask):
    count = lax.axis_size(axis)
    return lax.ppermute(value, axis, [(source, source ^ mask) for source in range(count)])


def added(*terms):
    terms = [term.astype(F32) for term in terms]
    while len(terms) > 1:
        terms = [terms[at] + terms[at + 1] for at in range(0, len(terms), 2)]
    return terms[0].astype(BF16)


def on_device(
    features, dw_kernel, dw_bias, ln_gain, ln_bias, w_in, b_in, w_out, b_out, layer_scale, cotangent
):
    quarter = (2 * lax.axis_index("x") + lax.axis_index("space") % 2).astype(jnp.uint32)
    turns = [quarter ^ turn for turn in range(4)]
    features, *turns = lax.optimization_barrier((features, *turns))
    x = jnp.swapaxes(features[0, 0], 1, 2)
    g = jnp.swapaxes(cotangent[0, 0], 1, 2)
    rows, chans, width = x.shape
    hidden_units = w_in.shape[1]
    strips = lax.axis_size("space")
    narrow = jax.ShapeDtypeStruct((REACH, chans, width), BF16)
    image = jax.ShapeDtypeStruct((rows, chans, width), BF16)

    def edge(first):
        return pl.pallas_call(
            lambda *refs: edge_kernel(*refs, first=first),
            out_shape=narrow,
            in_specs=[IN_VMEM],
            out_specs=IN_VMEM,
            compiler_params=SMALL,
        )(x)

    def first_swap(value):
        return swap(value, "space", 1)

    def second_swap(value):
        pairs = [(low, low + 1) for low in range(1, strips - 1, 2)]
        return lax.ppermute(value, "space", pairs + [(high, low) for low, high in pairs])

    first_halo = first_swap(edge(True))
    devices = lax.axis_size("x") * lax.axis_size("core") * strips
    scale = float(devices * rows * width) ** (-0.5)
    groups = chans // GROUP
    span = TAPS * GROUP
    inner = rows - 2 * REACH

    tall = jax.ShapeDtypeStruct((3 * REACH, chans, width), BF16)

    def kept(count):
        small = jax.ShapeDtypeStruct((count, chans, width), BF16)
        large = jax.ShapeDtypeStruct((count, hidden_units, width), BF16)
        return (small, large, small, large)

    def scratch(shapes):
        return [pltpu.VMEM(shape.shape, shape.dtype) for shape in shapes]

    middle = jax.ShapeDtypeStruct((inner, chans, width), BF16)
    spread = jax.ShapeDtypeStruct((groups, span, 2 * span), BF16)
    matrix = jax.ShapeDtypeStruct((chans, hidden_units), F32)
    terms = (matrix, matrix, jax.ShapeDtypeStruct((groups, 8, span), F32))
    vectors = (dw_bias, ln_gain, ln_bias, b_out, layer_scale)
    across_lanes = jax.ShapeDtypeStruct((len(vectors), chans, 128), F32)
    hidden_lanes = jax.ShapeDtypeStruct((hidden_units, 128), F32)
    turned = jax.ShapeDtypeStruct((hidden_units, chans), BF16)
    taps, back_taps, vectors, bias, w_in_t, w_out_turned = pl.pallas_call(
        prepare_kernel,
        out_shape=(spread, spread, across_lanes, hidden_lanes, turned, turned),
        in_specs=[IN_VMEM] * (4 + len(vectors)),
        out_specs=(IN_VMEM,) * 6,
        compiler_params=SMALL,
    )(dw_kernel, w_in, w_out.T, b_in.reshape(-1, 128), *[vector[None] for vector in vectors])
    weights = (vectors, bias, w_in, w_in_t, w_out_turned, w_out.T)
    out_inner, gz_inner, *inner_terms = pl.pallas_call(
        inner_kernel,
        out_shape=(middle, middle, *terms),
        in_specs=[IN_VMEM] * 9,
        out_specs=(IN_VMEM,) * 5,
        scratch_shapes=scratch(kept(inner)),
        compiler_params=PARAMS,
    )(x, g, taps, *weights)
    second_edge, out_inner = lax.optimization_barrier((edge(False), out_inner))
    second_halo = second_swap(second_edge)
    half_rows = hidden_units // 128 * chans + groups // 2 * 8
    half_rows = (half_rows + 63) // 64 * 64
    half = jax.ShapeDtypeStruct((half_rows, 128), BF16)
    out_first, gz_first, *first_terms = pl.pallas_call(
        first_kernel,
        out_shape=(narrow, narrow, *terms),
        in_specs=[IN_VMEM] * 13,
        out_specs=(IN_VMEM,) * 5,
        scratch_shapes=scratch((tall, *kept(REACH))),
        compiler_params=PARAMS,
    )(x, first_halo, g, taps, *weights, *inner_terms)
    gz_first_halo = first_swap(gz_first)
    out_second, gz_second, *second_kept = pl.pallas_call(
        second_kernel,
        out_shape=(narrow, narrow, tall, *kept(REACH)),
        in_specs=[IN_VMEM] * 10,
        out_specs=(IN_VMEM,) * 7,
        compiler_params=PARAMS,
    )(x, second_halo, g, taps, *weights)
    gz_second_halo = second_swap(gz_second)
    keep, send = pl.pallas_call(
        lambda *refs: terms_kernel(*refs, scale=scale),
        out_shape=(half, half),
        in_specs=[IN_VMEM] * 9,
        out_specs=(IN_VMEM,) * 2,
        scratch_shapes=[pltpu.VMEM((2, half_rows, 128), BF16)],
        compiler_params=PARAMS,
    )(second_kept[0], gz_second, *second_kept[1:], *first_terms)
    keep, send, gz_first_halo = lax.optimization_barrier((keep, send, gz_first_halo))

    summed = added(keep, swap(send, "core", 1)).reshape(4, half_rows // 4, 128)

    def at(turn):
        return lax.dynamic_index_in_dim(summed, turns[turn], 0, keepdims=False)

    def partner(value, turn):
        return swap(value, ("x", "space"), (turn >> 1) * strips | (turn & 1))

    own = added(at(0), *[partner(at(turn), turn) for turn in (1, 2, 3)])
    out, grad_rest = pl.pallas_call(
        input_kernel,
        out_shape=(image, image),
        in_specs=[IN_VMEM] * 9,
        out_specs=(IN_VMEM, IN_VMEM),
        scratch_shapes=[pltpu.VMEM((rows + REACH, chans, width), BF16)],
        compiler_params=PARAMS,
    )(out_first, out_inner, out_second, gz_first, gz_inner, gz_second, gz_first_halo, g, back_taps)
    bit = 2
    while bit < strips:
        masks = (bit, 2 * bit, 3 * bit) if 2 * bit < strips else (bit,)
        own = added(own, *[swap(own, "space", mask) for mask in masks])
        bit *= 4
    own, grad_rest = lax.optimization_barrier((own, grad_rest))
    mine = jnp.stack([own] + [partner(own, turn) for turn in (1, 2, 3)])
    grad_input = pl.pallas_call(
        input_rest_kernel,
        out_shape=image,
        in_specs=[IN_VMEM] * 6 + [pl.BlockSpec(memory_space=pl.ANY)],
        out_specs=pl.BlockSpec(memory_space=pl.ANY),
        scratch_shapes=[
            pltpu.VMEM((3 * REACH, chans, width), BF16),
            pltpu.VMEM((REACH, chans, width), BF16),
            pltpu.SemaphoreType.DMA(()),
        ],
        input_output_aliases={6: 0},
        compiler_params=PARAMS,
    )(gz_second_halo, gz_first, gz_inner, gz_second, g, back_taps, grad_rest)
    mine, grad_input = lax.optimization_barrier((mine, grad_input))
    other = swap(mine, "core", 1)
    grad_w_in, grad_w_out_t, grad_kernel = pl.pallas_call(
        final_kernel,
        out_shape=(matrix, matrix, jax.ShapeDtypeStruct((TAPS, TAPS, chans), F32)),
        in_specs=[IN_VMEM, IN_VMEM],
        out_specs=(IN_VMEM,) * 3,
        scratch_shapes=[pltpu.VMEM((2, half_rows, 128), BF16)],
        compiler_params=PARAMS,
    )(mine, other)
    block_output = jnp.swapaxes(out, 1, 2)[None, None]
    grad_image = jnp.swapaxes(grad_input, 1, 2)[None, None]
    return (block_output, grad_image, grad_w_in, grad_w_out_t.T, grad_kernel)


def solution(mesh):
    slides, strips = mesh.devices.shape
    split = Mesh(mesh.devices.reshape(slides // 2, 2, strips), ("x", "core", "space"))
    placed = P(("x", "core"), "space", None, None, None)
    return jax.shard_map(
        on_device,
        mesh=split,
        in_specs=(placed,) + (P(),) * 9 + (placed,),
        out_specs=(placed, placed, P(), P(), P()),
        check_vma=False,
    )
```

```python
import jax
import jax.numpy as jnp
from jax import lax
from jax.experimental import pallas as pl
from jax.experimental.pallas import tpu as pltpu
from jax.sharding import Mesh
from jax.sharding import PartitionSpec as P

EPSILON = 1e-06
TAPS = 7
REACH = 3
GROUP = 16
BF16 = jnp.bfloat16
F32 = jnp.float32


def slide_lanes(value, steps):
    if steps == 0:
        return value
    width = value.shape[-1]
    lane = lax.broadcasted_iota(jnp.int32, value.shape, value.ndim - 1)
    moved = pltpu.roll(value, (-steps) % width, value.ndim - 1)
    keep = lane < width - steps if steps > 0 else lane >= -steps
    return jnp.where(keep, moved, jnp.zeros_like(moved))


def conv_row(tall_ref, taps_ref, row):
    _, chans, width = tall_ref.shape
    pieces = []
    for group in range(chans // GROUP):
        window = tall_ref[pl.ds(row, TAPS), group * GROUP : (group + 1) * GROUP, :]
        window = window.reshape(TAPS * GROUP, width)
        window = jnp.concatenate([window, window], axis=0)
        parts = jnp.dot(taps_ref[group], window, preferred_element_type=F32)
        total = None
        for tap in range(TAPS):
            part = slide_lanes(parts[tap * GROUP : (tap + 1) * GROUP], tap - REACH)
            total = part if total is None else total + part
        pieces.append(total)
    return jnp.concatenate(pieces, axis=0)


def is_low():
    return 1 - lax.axis_index("space") % 2


def spread_taps(kernel_ref, taps_ref, flipped):
    chans = kernel_ref.shape[2]
    span = TAPS * GROUP
    same = lax.broadcasted_iota(jnp.int32, (GROUP, span), 0) == lax.broadcasted_iota(
        jnp.int32, (GROUP, span), 1
    ) % GROUP
    for group in range(chans // GROUP):
        lanes = slice(group * GROUP, (group + 1) * GROUP)
        order = [TAPS - 1 - tap if flipped else tap for tap in range(TAPS)]
        across = jnp.concatenate([kernel_ref[tap, :, lanes] for tap in order], axis=1)
        for tap in range(TAPS):
            source = TAPS - 1 - tap if flipped else tap
            wide = jnp.broadcast_to(across[source : source + 1], (GROUP, span))
            wide = jnp.where(same, wide, 0.0)
            high = wide.astype(BF16)
            low = (wide - high.astype(F32)).astype(BF16)
            taps_ref[group, tap * GROUP : (tap + 1) * GROUP, :] = jnp.concatenate([high, low], axis=1)


def one_row(row, tall_ref, g_ref, taps_ref, weights, out_ref, gz_ref, kept):
    vec_ref, bin_ref, win_ref, wint_ref, wout_ref, woutt_ref = weights
    normed_ref, act_ref, gout_ref, gh_ref = kept

    width = g_ref.shape[2]

    def vec(index):
        return across(vec_ref[index], width)

    hidden_units = win_ref.shape[1]
    mixed = conv_row(tall_ref, taps_ref, row) + vec(0)
    centre = mixed - jnp.mean(mixed, axis=0, keepdims=True)
    inverse = lax.rsqrt(jnp.mean(centre * centre, axis=0, keepdims=True) + EPSILON)
    unit = centre * inverse
    normed = (unit * vec(1) + vec(2)).astype(BF16)
    normed_ref[row] = normed
    gout = (vec(4) * g_ref[row].astype(F32)).astype(BF16)
    gout_ref[row] = gout
    span = 256
    for start in range(0, hidden_units, span):
        part = slice(start, start + span)
        hidden = jnp.dot(wint_ref[part, :], normed, preferred_element_type=F32) + across(bin_ref[part, :], width)
        grad_act = jnp.dot(wout_ref[part, :], gout, preferred_element_type=F32)
        cdf = 0.5 * (1.0 + lax.erf(hidden * 0.7071067811865476))
        slope = cdf + hidden * jnp.exp(-0.5 * hidden * hidden) * 0.3989422804014327
        act_ref[row, part, :] = (hidden * cdf).astype(BF16)
        gh_ref[row, part, :] = (grad_act * slope).astype(BF16)
    branch = jnp.dot(woutt_ref[...], act_ref[row], preferred_element_type=F32) + vec(3)
    out_ref[row] = (tall_ref[row + REACH].astype(F32) + vec(4) * branch).astype(BF16)
    grad_norm = jnp.dot(win_ref[...], gh_ref[row], preferred_element_type=F32) * vec(1)
    grad_mixed = inverse * (
        grad_norm
        - jnp.mean(grad_norm, axis=0, keepdims=True)
        - unit * jnp.mean(grad_norm * unit, axis=0, keepdims=True)
    )
    gz_ref[row] = grad_mixed.astype(BF16)


def all_rows(tall_ref, g_ref, taps_ref, weights, out_ref, gz_ref, kept):
    def step(row, carry):
        one_row(row, tall_ref, g_ref, taps_ref, weights, out_ref, gz_ref, kept)
        return carry

    lax.fori_loop(0, out_ref.shape[0], step, 0, unroll=True)


NT = (((1,), (1,)), ((), ()))


def total_of(terms):
    total = terms[0]
    for term in terms[1:]:
        total = total + term
    return total


def weight_terms(kept, start, width, index):
    normed_ref, act_ref, gout_ref, gh_ref = kept
    left, right = ((normed_ref, gh_ref), (gout_ref, act_ref))[index]
    return total_of(
        [
            lax.dot_general(left[row], right[row, start : start + width, :], NT, preferred_element_type=F32)
            for row in range(left.shape[0])
        ]
    )


def tap_terms(tall_ref, gz_ref, group):
    span = TAPS * GROUP
    same = lax.broadcasted_iota(jnp.int32, (span, span), 0) % GROUP == lax.broadcasted_iota(
        jnp.int32, (span, span), 1
    ) % GROUP
    lanes = slice(group * GROUP, (group + 1) * GROUP)
    terms = []
    for row in range(gz_ref.shape[0]):
        grad = gz_ref[row, lanes, :].astype(F32)
        moved = jnp.concatenate([slide_lanes(grad, REACH - tap) for tap in range(TAPS)], axis=0).astype(BF16)
        window = tall_ref[row : row + TAPS, lanes, :].reshape(span, -1)
        terms.append(lax.dot_general(moved, window, NT, preferred_element_type=F32))
    total = jnp.where(same, total_of(terms), 0.0)
    summed = jnp.sum(total.reshape(TAPS, GROUP, span), axis=1)
    return jnp.concatenate([summed, jnp.zeros((1, span), F32)], axis=0)


def prepare_kernel(
    kernel_ref, win_ref, woutt_ref, bin_in_ref, *refs
):
    count = len(refs) - 5
    vectors, (taps_ref, vec_ref, bin_ref, wint_ref, wout_ref) = refs[:count], refs[count:]
    spread_taps(kernel_ref, taps_ref, False)
    for source, target in ((win_ref, wint_ref), (woutt_ref, wout_ref)):
        target[...] = source[...].T
    chans = vec_ref.shape[1]
    for index, ref in enumerate(vectors):
        row = jnp.concatenate([ref[...], jnp.zeros((1, -chans % 128), F32)], axis=1)
        for start in range(0, chans, 128):
            size = min(128, chans - start)
            square = jnp.broadcast_to(row[:, start : start + 128], (128, 128)).T
            vec_ref[index, start : start + size, :] = square[:size]
    for index in range(bin_in_ref.shape[0]):
        square = jnp.broadcast_to(bin_in_ref[index : index + 1, :], (128, 128))
        bin_ref[index * 128 : (index + 1) * 128, :] = square.T


def across(value, width):
    return jnp.concatenate([value] * (width // 128), axis=1)


def inner_kernel(
    x_ref, g_ref, taps_ref, vec_ref, bin_ref, win_ref, wint_ref, wout_ref, woutt_ref,
    out_ref, gz_ref, dwin_ref, dwout_ref, dtaps_ref,
    *kept,
):
    hidden_units = win_ref.shape[1]
    weights = (vec_ref, bin_ref, win_ref, wint_ref, wout_ref, woutt_ref)
    all_rows(x_ref, g_ref.at[pl.ds(REACH, out_ref.shape[0])], taps_ref, weights, out_ref, gz_ref, kept)
    for start in range(0, hidden_units, 256):
        for index, ref in enumerate((dwin_ref, dwout_ref)):
            ref[:, start : start + 256] = weight_terms(kept, start, 256, index)
    for group in range(x_ref.shape[1] // GROUP):
        dtaps_ref[group] = tap_terms(x_ref, gz_ref, group)


def with_halo(x_ref, halo_ref, tall_ref, low):
    shared = 2 * REACH
    tall_ref[pl.ds(shared * low, REACH)] = halo_ref[...]
    tall_ref[pl.ds(REACH * (1 - low), shared)] = x_ref[pl.ds((x_ref.shape[0] - shared) * low, shared)]


def first_kernel(
    x_ref, halo_ref, g_ref, taps_ref, vec_ref, bin_ref, win_ref, wint_ref, wout_ref, woutt_ref,
    dwin_in_ref, dwout_in_ref, dtaps_in_ref,
    out_ref, gz_ref, dwin_ref, dwout_ref, dtaps_ref,
    tall_ref, *kept,
):
    hidden_units = win_ref.shape[1]
    low = is_low()
    with_halo(x_ref, halo_ref, tall_ref, low)
    weights = (vec_ref, bin_ref, win_ref, wint_ref, wout_ref, woutt_ref)
    rows = g_ref.at[pl.ds((x_ref.shape[0] - REACH) * low, REACH)]
    all_rows(tall_ref, rows, taps_ref, weights, out_ref, gz_ref, kept)
    for start in range(0, hidden_units, 256):
        part = slice(start, start + 256)
        for index, (ref, before_ref) in enumerate(((dwin_ref, dwin_in_ref), (dwout_ref, dwout_in_ref))):
            ref[:, part] = weight_terms(kept, start, 256, index) + before_ref[:, part]
    for group in range(x_ref.shape[1] // GROUP):
        dtaps_ref[group] = tap_terms(tall_ref, gz_ref, group) + dtaps_in_ref[group]


def second_kernel(
    x_ref, halo_ref, g_ref, taps_ref, vec_ref, bin_ref, win_ref, wint_ref, wout_ref, woutt_ref,
    out_ref, gz_ref, tall_ref, *kept,
):
    low = 1 - is_low()
    with_halo(x_ref, halo_ref, tall_ref, low)
    weights = (vec_ref, bin_ref, win_ref, wint_ref, wout_ref, woutt_ref)
    rows = g_ref.at[pl.ds((x_ref.shape[0] - REACH) * low, REACH)]
    all_rows(tall_ref, rows, taps_ref, weights, out_ref, gz_ref, kept)


def terms_kernel(
    tall_ref, gz_ref, normed_ref, act_ref, gout_ref, gh_ref, dwin_ref, dwout_ref, dtaps_ref,
    keep_ref, send_ref, halves_ref, *, scale,
):
    chans, hidden_units = dwin_ref.shape
    kept = (normed_ref, act_ref, gout_ref, gh_ref)
    blocks = hidden_units // 128
    for index, ref in enumerate((dwin_ref, dwout_ref)):
        for start in range(0, hidden_units, 256):
            total = (weight_terms(kept, start, 256, index) + ref[:, start : start + 256]) * scale
            for lanes in range(2):
                block = start // 128 + lanes
                halves_ref[index, block * chans : (block + 1) * chans, :] = total[
                    :, lanes * 128 : (lanes + 1) * 128
                ].astype(BF16)
    at = blocks * chans
    groups = chans // GROUP
    halves_ref[:, at:, :] = jnp.zeros((2, halves_ref.shape[1] - at, 128), BF16)
    span = TAPS * GROUP
    for pair in range(groups // 2):
        both = [
            (tap_terms(tall_ref, gz_ref, group) + dtaps_ref[group]) * scale for group in (2 * pair, 2 * pair + 1)
        ]
        both = jnp.concatenate(both, axis=0)
        both = jnp.concatenate([both, jnp.zeros((16, 128 - span), F32)], axis=1)
        half, place = divmod(pair, groups // 4)
        halves_ref[half, at + place * 16 : at + (place + 1) * 16, :] = both.astype(BF16)
    core = lax.axis_index("core")
    keep_ref[...] = halves_ref[core]
    send_ref[...] = halves_ref[1 - core]


def input_kernel(
    out_first_ref, out_inner_ref, out_second_ref, gz_first_ref, gz_inner_ref, gz_second_ref,
    halo_ref, g_ref, kernel_ref,
    out_ref, grad_ref, taps_ref, tall_ref,
):
    spread_taps(kernel_ref, taps_ref, True)
    low = is_low()
    rows = g_ref.shape[0]
    inner = rows - 2 * REACH
    tall_ref[pl.ds(rows * (1 - low), REACH)] = gz_second_ref[...]
    tall_ref[pl.ds(REACH * (2 - low), inner)] = gz_inner_ref[...]
    tall_ref[pl.ds(REACH + inner * low, REACH)] = gz_first_ref[...]
    tall_ref[pl.ds(rows * low, REACH)] = halo_ref[...]
    out_ref[REACH : REACH + inner] = out_inner_ref[...]
    out_ref[pl.ds((rows - REACH) * low, REACH)] = out_first_ref[...]
    out_ref[pl.ds((rows - REACH) * (1 - low), REACH)] = out_second_ref[...]

    def step(row, carry):
        at = row + REACH * low
        grad_ref[at] = (g_ref[at].astype(F32) + conv_row(tall_ref, taps_ref, row)).astype(BF16)
        return carry

    lax.fori_loop(0, rows - REACH, step, 0)


def input_rest_kernel(
    halo_ref, gz_first_ref, gz_inner_ref, gz_second_ref, g_ref, taps_ref, rest_ref,
    grad_ref, tall_ref, part_ref, sem,
):
    low = 1 - is_low()
    rows = g_ref.shape[0]
    inner = rows - 2 * REACH
    near = REACH - inner
    tall_ref[pl.ds(2 * REACH * low, REACH)] = halo_ref[...]
    tall_ref[REACH : 2 * REACH] = gz_second_ref[...]
    tall_ref[pl.ds(2 * REACH * (1 - low) + near * low, inner)] = gz_inner_ref[...]
    tall_ref[pl.ds((2 * REACH + inner) * (1 - low), near)] = gz_first_ref[pl.ds((REACH - near) * low, near)]
    first = (rows - REACH) * low

    def step(row, carry):
        part_ref[row] = (g_ref[first + row].astype(F32) + conv_row(tall_ref, taps_ref, row)).astype(BF16)
        return carry

    lax.fori_loop(0, REACH, step, 0)
    copy = pltpu.make_async_copy(part_ref, grad_ref.at[pl.ds(first, REACH)], sem)
    copy.start()
    copy.wait()


def final_kernel(mine_ref, other_ref, win_ref, woutt_ref, taps_ref, all_ref):
    core = lax.axis_index("core")
    quarter = 2 * lax.axis_index("x") + lax.axis_index("space") % 2
    chans, hidden_units = win_ref.shape
    size = mine_ref.shape[1]
    for turn in range(4):
        at = pl.ds(pl.multiple_of((quarter ^ turn) * size, 16), size)
        all_ref[core, at, :] = mine_ref[turn]
        all_ref[1 - core, at, :] = other_ref[turn]
    blocks = hidden_units // 128
    for index, ref in enumerate((win_ref, woutt_ref)):
        for block in range(blocks):
            ref[:, block * 128 : (block + 1) * 128] = all_ref[index, block * chans : (block + 1) * chans, :].astype(F32)
    groups = chans // GROUP
    for pair in range(groups // 2):
        half, place = divmod(pair, groups // 4)
        at = blocks * chans + place * 16
        both = all_ref[half, at : at + 16, :].astype(F32)
        for side in range(2):
            group = 2 * pair + side
            piece = both[side * 8 : side * 8 + 8]
            for tap in range(TAPS):
                taps_ref[tap, :, group * GROUP : (group + 1) * GROUP] = piece[:TAPS, tap * GROUP : (tap + 1) * GROUP]


def edge_kernel(x_ref, edge_ref, *, first):
    low = is_low() if first else 1 - is_low()
    edge_ref[...] = x_ref[pl.ds((x_ref.shape[0] - REACH) * low, REACH)]


PARAMS = pltpu.CompilerParams(vmem_limit_bytes=20 * 1024 * 1024)
SMALL = pltpu.CompilerParams(vmem_limit_bytes=8 * 1024 * 1024)
IN_VMEM = pl.BlockSpec(memory_space=pltpu.VMEM)


def swap(value, axis, mask):
    count = lax.axis_size(axis)
    return lax.ppermute(value, axis, [(source, source ^ mask) for source in range(count)])


def added(*terms):
    terms = [term.astype(F32) for term in terms]
    while len(terms) > 1:
        terms = [terms[at] + terms[at + 1] for at in range(0, len(terms), 2)]
    return terms[0].astype(BF16)


def on_device(
    features, dw_kernel, dw_bias, ln_gain, ln_bias, w_in, b_in, w_out, b_out, layer_scale, cotangent
):
    quarter = (2 * lax.axis_index("x") + lax.axis_index("space") % 2).astype(jnp.uint32)
    turns = [quarter ^ turn for turn in range(4)]
    features, *turns = lax.optimization_barrier((features, *turns))
    x = jnp.swapaxes(features[0, 0], 1, 2)
    g = jnp.swapaxes(cotangent[0, 0], 1, 2)
    rows, chans, width = x.shape
    hidden_units = w_in.shape[1]
    strips = lax.axis_size("space")
    narrow = jax.ShapeDtypeStruct((REACH, chans, width), BF16)
    image = jax.ShapeDtypeStruct((rows, chans, width), BF16)

    def edge(first):
        return pl.pallas_call(
            lambda *refs: edge_kernel(*refs, first=first),
            out_shape=narrow,
            in_specs=[IN_VMEM],
            out_specs=IN_VMEM,
            compiler_params=SMALL,
        )(x)

    def first_swap(value):
        return swap(value, "space", 1)

    def second_swap(value):
        pairs = [(low, low + 1) for low in range(1, strips - 1, 2)]
        return lax.ppermute(value, "space", pairs + [(high, low) for low, high in pairs])

    first_halo = first_swap(edge(True))
    devices = lax.axis_size("x") * lax.axis_size("core") * strips
    scale = float(devices * rows * width) ** (-0.5)
    groups = chans // GROUP
    span = TAPS * GROUP
    inner = rows - 2 * REACH

    tall = jax.ShapeDtypeStruct((3 * REACH, chans, width), BF16)

    def kept(count):
        small = jax.ShapeDtypeStruct((count, chans, width), BF16)
        large = jax.ShapeDtypeStruct((count, hidden_units, width), BF16)
        return (small, large, small, large)

    def scratch(shapes):
        return [pltpu.VMEM(shape.shape, shape.dtype) for shape in shapes]

    middle = jax.ShapeDtypeStruct((inner, chans, width), BF16)
    spread = jax.ShapeDtypeStruct((groups, span, 2 * span), BF16)
    matrix = jax.ShapeDtypeStruct((chans, hidden_units), F32)
    terms = (matrix, matrix, jax.ShapeDtypeStruct((groups, 8, span), F32))
    vectors = (dw_bias, ln_gain, ln_bias, b_out, layer_scale)
    across_lanes = jax.ShapeDtypeStruct((len(vectors), chans, 128), F32)
    hidden_lanes = jax.ShapeDtypeStruct((hidden_units, 128), F32)
    turned = jax.ShapeDtypeStruct((hidden_units, chans), BF16)
    taps, vectors, bias, w_in_t, w_out_turned = pl.pallas_call(
        prepare_kernel,
        out_shape=(spread, across_lanes, hidden_lanes, turned, turned),
        in_specs=[IN_VMEM] * (4 + len(vectors)),
        out_specs=(IN_VMEM,) * 5,
        compiler_params=SMALL,
    )(dw_kernel, w_in, w_out.T, b_in.reshape(-1, 128), *[vector[None] for vector in vectors])
    weights = (vectors, bias, w_in, w_in_t, w_out_turned, w_out.T)
    out_inner, gz_inner, *inner_terms = pl.pallas_call(
        inner_kernel,
        out_shape=(middle, middle, *terms),
        in_specs=[IN_VMEM] * 9,
        out_specs=(IN_VMEM,) * 5,
        scratch_shapes=scratch(kept(inner)),
        compiler_params=PARAMS,
    )(x, g, taps, *weights)
    second_edge, out_inner = lax.optimization_barrier((edge(False), out_inner))
    second_halo = second_swap(second_edge)
    half_rows = hidden_units // 128 * chans + groups // 2 * 8
    half_rows = (half_rows + 63) // 64 * 64
    half = jax.ShapeDtypeStruct((half_rows, 128), BF16)
    out_first, gz_first, *first_terms = pl.pallas_call(
        first_kernel,
        out_shape=(narrow, narrow, *terms),
        in_specs=[IN_VMEM] * 13,
        out_specs=(IN_VMEM,) * 5,
        scratch_shapes=scratch((tall, *kept(REACH))),
        compiler_params=PARAMS,
    )(x, first_halo, g, taps, *weights, *inner_terms)
    gz_first_halo = first_swap(gz_first)
    out_second, gz_second, *second_kept = pl.pallas_call(
        second_kernel,
        out_shape=(narrow, narrow, tall, *kept(REACH)),
        in_specs=[IN_VMEM] * 10,
        out_specs=(IN_VMEM,) * 7,
        compiler_params=PARAMS,
    )(x, second_halo, g, taps, *weights)
    gz_second_halo = second_swap(gz_second)
    keep, send = pl.pallas_call(
        lambda *refs: terms_kernel(*refs, scale=scale),
        out_shape=(half, half),
        in_specs=[IN_VMEM] * 9,
        out_specs=(IN_VMEM,) * 2,
        scratch_shapes=[pltpu.VMEM((2, half_rows, 128), BF16)],
        compiler_params=PARAMS,
    )(second_kept[0], gz_second, *second_kept[1:], *first_terms)
    keep, send, gz_first_halo = lax.optimization_barrier((keep, send, gz_first_halo))

    summed = added(keep, swap(send, "core", 1)).reshape(4, half_rows // 4, 128)

    def at(turn):
        return lax.dynamic_index_in_dim(summed, turns[turn], 0, keepdims=False)

    def partner(value, turn):
        return swap(value, ("x", "space"), (turn >> 1) * strips | (turn & 1))

    own = added(at(0), *[partner(at(turn), turn) for turn in (1, 2, 3)])
    out, grad_rest, back_taps = pl.pallas_call(
        input_kernel,
        out_shape=(image, image, spread),
        in_specs=[IN_VMEM] * 9,
        out_specs=(IN_VMEM,) * 3,
        scratch_shapes=[pltpu.VMEM((rows + REACH, chans, width), BF16)],
        compiler_params=PARAMS,
    )(out_first, out_inner, out_second, gz_first, gz_inner, gz_second, gz_first_halo, g, dw_kernel)
    bit = 2
    while bit < strips:
        masks = (bit, 2 * bit, 3 * bit) if 2 * bit < strips else (bit,)
        own = added(own, *[swap(own, "space", mask) for mask in masks])
        bit *= 4
    own, grad_rest = lax.optimization_barrier((own, grad_rest))
    mine = jnp.stack([own] + [partner(own, turn) for turn in (1, 2, 3)])
    grad_input = pl.pallas_call(
        input_rest_kernel,
        out_shape=image,
        in_specs=[IN_VMEM] * 6 + [pl.BlockSpec(memory_space=pl.ANY)],
        out_specs=pl.BlockSpec(memory_space=pl.ANY),
        scratch_shapes=[
            pltpu.VMEM((3 * REACH, chans, width), BF16),
            pltpu.VMEM((REACH, chans, width), BF16),
            pltpu.SemaphoreType.DMA(()),
        ],
        input_output_aliases={6: 0},
        compiler_params=PARAMS,
    )(gz_second_halo, gz_first, gz_inner, gz_second, g, back_taps, grad_rest)
    mine, grad_input = lax.optimization_barrier((mine, grad_input))
    other = swap(mine, "core", 1)
    grad_w_in, grad_w_out_t, grad_kernel = pl.pallas_call(
        final_kernel,
        out_shape=(matrix, matrix, jax.ShapeDtypeStruct((TAPS, TAPS, chans), F32)),
        in_specs=[IN_VMEM, IN_VMEM],
        out_specs=(IN_VMEM,) * 3,
        scratch_shapes=[pltpu.VMEM((2, half_rows, 128), BF16)],
        compiler_params=PARAMS,
    )(mine, other)
    block_output = jnp.swapaxes(out, 1, 2)[None, None]
    grad_image = jnp.swapaxes(grad_input, 1, 2)[None, None]
    return (block_output, grad_image, grad_w_in, grad_w_out_t.T, grad_kernel)


def solution(mesh):
    slides, strips = mesh.devices.shape
    split = Mesh(mesh.devices.reshape(slides // 2, 2, strips), ("x", "core", "space"))
    placed = P(("x", "core"), "space", None, None, None)
    return jax.shard_map(
        on_device,
        mesh=split,
        in_specs=(placed,) + (P(),) * 9 + (placed,),
        out_specs=(placed, placed, P(), P(), P()),
        check_vma=False,
    )
```

```python
import jax
import jax.numpy as jnp
from jax import lax
from jax.experimental import pallas as pl
from jax.experimental.pallas import tpu as pltpu
from jax.sharding import Mesh
from jax.sharding import PartitionSpec as P

EPSILON = 1e-06
TAPS = 7
REACH = 3
GROUP = 16
BF16 = jnp.bfloat16
F32 = jnp.float32


def slide_lanes(value, steps):
    if steps == 0:
        return value
    width = value.shape[-1]
    lane = lax.broadcasted_iota(jnp.int32, value.shape, value.ndim - 1)
    moved = pltpu.roll(value, (-steps) % width, value.ndim - 1)
    keep = lane < width - steps if steps > 0 else lane >= -steps
    return jnp.where(keep, moved, jnp.zeros_like(moved))


def conv_row(tall_ref, taps_ref, row):
    _, chans, width = tall_ref.shape
    pieces = []
    for group in range(chans // GROUP):
        window = tall_ref[pl.ds(row, TAPS), group * GROUP : (group + 1) * GROUP, :]
        window = window.reshape(TAPS * GROUP, width)
        window = jnp.concatenate([window, window], axis=0)
        parts = jnp.dot(taps_ref[group], window, preferred_element_type=F32)
        total = None
        for tap in range(TAPS):
            part = slide_lanes(parts[tap * GROUP : (tap + 1) * GROUP], tap - REACH)
            total = part if total is None else total + part
        pieces.append(total)
    return jnp.concatenate(pieces, axis=0)


def is_low():
    return 1 - lax.axis_index("space") % 2


def spread_taps(kernel_ref, taps_ref, flipped):
    chans = kernel_ref.shape[2]
    span = TAPS * GROUP
    same = lax.broadcasted_iota(jnp.int32, (GROUP, span), 0) == lax.broadcasted_iota(
        jnp.int32, (GROUP, span), 1
    ) % GROUP
    for group in range(chans // GROUP):
        lanes = slice(group * GROUP, (group + 1) * GROUP)
        order = [TAPS - 1 - tap if flipped else tap for tap in range(TAPS)]
        across = jnp.concatenate([kernel_ref[tap, :, lanes] for tap in order], axis=1)
        for tap in range(TAPS):
            source = TAPS - 1 - tap if flipped else tap
            wide = jnp.broadcast_to(across[source : source + 1], (GROUP, span))
            wide = jnp.where(same, wide, 0.0)
            high = wide.astype(BF16)
            low = (wide - high.astype(F32)).astype(BF16)
            taps_ref[group, tap * GROUP : (tap + 1) * GROUP, :] = jnp.concatenate([high, low], axis=1)


def one_row(row, tall_ref, g_ref, taps_ref, weights, out_ref, gz_ref, kept):
    vec_ref, bin_ref, win_ref, wint_ref, wout_ref, woutt_ref = weights
    normed_ref, act_ref, gout_ref, gh_ref = kept

    width = g_ref.shape[2]

    def vec(index):
        return across(vec_ref[index], width)

    hidden_units = win_ref.shape[1]
    mixed = conv_row(tall_ref, taps_ref, row) + vec(0)
    centre = mixed - jnp.mean(mixed, axis=0, keepdims=True)
    inverse = lax.rsqrt(jnp.mean(centre * centre, axis=0, keepdims=True) + EPSILON)
    unit = centre * inverse
    normed = (unit * vec(1) + vec(2)).astype(BF16)
    normed_ref[row] = normed
    gout = (vec(4) * g_ref[row].astype(F32)).astype(BF16)
    gout_ref[row] = gout
    span = 256
    for start in range(0, hidden_units, span):
        part = slice(start, start + span)
        hidden = jnp.dot(wint_ref[part, :], normed, preferred_element_type=F32) + across(bin_ref[part, :], width)
        grad_act = jnp.dot(wout_ref[part, :], gout, preferred_element_type=F32)
        cdf = 0.5 * (1.0 + lax.erf(hidden * 0.7071067811865476))
        slope = cdf + hidden * jnp.exp(-0.5 * hidden * hidden) * 0.3989422804014327
        act_ref[row, part, :] = (hidden * cdf).astype(BF16)
        gh_ref[row, part, :] = (grad_act * slope).astype(BF16)
    branch = jnp.dot(woutt_ref[...], act_ref[row], preferred_element_type=F32) + vec(3)
    out_ref[row] = (tall_ref[row + REACH].astype(F32) + vec(4) * branch).astype(BF16)
    grad_norm = jnp.dot(win_ref[...], gh_ref[row], preferred_element_type=F32) * vec(1)
    grad_mixed = inverse * (
        grad_norm
        - jnp.mean(grad_norm, axis=0, keepdims=True)
        - unit * jnp.mean(grad_norm * unit, axis=0, keepdims=True)
    )
    gz_ref[row] = grad_mixed.astype(BF16)


def all_rows(tall_ref, g_ref, taps_ref, weights, out_ref, gz_ref, kept):
    def step(row, carry):
        one_row(row, tall_ref, g_ref, taps_ref, weights, out_ref, gz_ref, kept)
        return carry

    lax.fori_loop(0, out_ref.shape[0], step, 0, unroll=True)


NT = (((1,), (1,)), ((), ()))


def total_of(terms):
    total = terms[0]
    for term in terms[1:]:
        total = total + term
    return total


def weight_terms(kept, start, width, index):
    normed_ref, act_ref, gout_ref, gh_ref = kept
    left, right = ((normed_ref, gh_ref), (gout_ref, act_ref))[index]
    return total_of(
        [
            lax.dot_general(left[row], right[row, start : start + width, :], NT, preferred_element_type=F32)
            for row in range(left.shape[0])
        ]
    )


def tap_terms(tall_ref, gz_ref, group):
    span = TAPS * GROUP
    same = lax.broadcasted_iota(jnp.int32, (span, span), 0) % GROUP == lax.broadcasted_iota(
        jnp.int32, (span, span), 1
    ) % GROUP
    lanes = slice(group * GROUP, (group + 1) * GROUP)
    terms = []
    for row in range(gz_ref.shape[0]):
        grad = gz_ref[row, lanes, :].astype(F32)
        moved = jnp.concatenate([slide_lanes(grad, REACH - tap) for tap in range(TAPS)], axis=0).astype(BF16)
        window = tall_ref[row : row + TAPS, lanes, :].reshape(span, -1)
        terms.append(lax.dot_general(moved, window, NT, preferred_element_type=F32))
    total = jnp.where(same, total_of(terms), 0.0)
    summed = jnp.sum(total.reshape(TAPS, GROUP, span), axis=1)
    return jnp.concatenate([summed, jnp.zeros((1, span), F32)], axis=0)


def prepare_kernel(
    kernel_ref, win_ref, woutt_ref, bin_in_ref, *refs
):
    count = len(refs) - 5
    vectors, (taps_ref, vec_ref, bin_ref, wint_ref, wout_ref) = refs[:count], refs[count:]
    spread_taps(kernel_ref, taps_ref, False)
    for source, target in ((win_ref, wint_ref), (woutt_ref, wout_ref)):
        target[...] = source[...].T
    chans = vec_ref.shape[1]
    for index, ref in enumerate(vectors):
        row = jnp.concatenate([ref[...], jnp.zeros((1, -chans % 128), F32)], axis=1)
        for start in range(0, chans, 128):
            size = min(128, chans - start)
            square = jnp.broadcast_to(row[:, start : start + 128], (128, 128)).T
            vec_ref[index, start : start + size, :] = square[:size]
    for index in range(bin_in_ref.shape[0]):
        square = jnp.broadcast_to(bin_in_ref[index : index + 1, :], (128, 128))
        bin_ref[index * 128 : (index + 1) * 128, :] = square.T


def across(value, width):
    return jnp.concatenate([value] * (width // 128), axis=1)


def inner_kernel(
    x_ref, g_ref, taps_ref, vec_ref, bin_ref, win_ref, wint_ref, wout_ref, woutt_ref,
    out_ref, gz_ref, dwin_ref, dwout_ref, dtaps_ref,
    *kept,
):
    hidden_units = win_ref.shape[1]
    weights = (vec_ref, bin_ref, win_ref, wint_ref, wout_ref, woutt_ref)
    all_rows(x_ref, g_ref.at[pl.ds(REACH, out_ref.shape[0])], taps_ref, weights, out_ref, gz_ref, kept)
    for start in range(0, hidden_units, 256):
        for index, ref in enumerate((dwin_ref, dwout_ref)):
            ref[:, start : start + 256] = weight_terms(kept, start, 256, index)
    for group in range(x_ref.shape[1] // GROUP):
        dtaps_ref[group] = tap_terms(x_ref, gz_ref, group)


def with_halo(x_ref, halo_ref, tall_ref, low):
    shared = 2 * REACH
    tall_ref[pl.ds(shared * low, REACH)] = halo_ref[...]
    tall_ref[pl.ds(REACH * (1 - low), shared)] = x_ref[pl.ds((x_ref.shape[0] - shared) * low, shared)]


def first_kernel(
    x_ref, halo_ref, g_ref, taps_ref, vec_ref, bin_ref, win_ref, wint_ref, wout_ref, woutt_ref,
    dwin_in_ref, dwout_in_ref, dtaps_in_ref,
    out_ref, gz_ref, dwin_ref, dwout_ref, dtaps_ref,
    tall_ref, *kept,
):
    hidden_units = win_ref.shape[1]
    low = is_low()
    with_halo(x_ref, halo_ref, tall_ref, low)
    weights = (vec_ref, bin_ref, win_ref, wint_ref, wout_ref, woutt_ref)
    rows = g_ref.at[pl.ds((x_ref.shape[0] - REACH) * low, REACH)]
    all_rows(tall_ref, rows, taps_ref, weights, out_ref, gz_ref, kept)
    for start in range(0, hidden_units, 256):
        part = slice(start, start + 256)
        for index, (ref, before_ref) in enumerate(((dwin_ref, dwin_in_ref), (dwout_ref, dwout_in_ref))):
            ref[:, part] = weight_terms(kept, start, 256, index) + before_ref[:, part]
    for group in range(x_ref.shape[1] // GROUP):
        dtaps_ref[group] = tap_terms(tall_ref, gz_ref, group) + dtaps_in_ref[group]


def second_kernel(
    x_ref, halo_ref, g_ref, taps_ref, vec_ref, bin_ref, win_ref, wint_ref, wout_ref, woutt_ref,
    out_ref, gz_ref, tall_ref, *kept,
):
    low = 1 - is_low()
    with_halo(x_ref, halo_ref, tall_ref, low)
    weights = (vec_ref, bin_ref, win_ref, wint_ref, wout_ref, woutt_ref)
    rows = g_ref.at[pl.ds((x_ref.shape[0] - REACH) * low, REACH)]
    all_rows(tall_ref, rows, taps_ref, weights, out_ref, gz_ref, kept)


def terms_kernel(
    tall_ref, gz_ref, normed_ref, act_ref, gout_ref, gh_ref, dwin_ref, dwout_ref, dtaps_ref,
    keep_ref, send_ref, halves_ref, *, scale,
):
    chans, hidden_units = dwin_ref.shape
    kept = (normed_ref, act_ref, gout_ref, gh_ref)
    blocks = hidden_units // 128
    for index, ref in enumerate((dwin_ref, dwout_ref)):
        for start in range(0, hidden_units, 256):
            total = (weight_terms(kept, start, 256, index) + ref[:, start : start + 256]) * scale
            for lanes in range(2):
                block = start // 128 + lanes
                halves_ref[index, block * chans : (block + 1) * chans, :] = total[
                    :, lanes * 128 : (lanes + 1) * 128
                ].astype(BF16)
    at = blocks * chans
    groups = chans // GROUP
    halves_ref[:, at:, :] = jnp.zeros((2, halves_ref.shape[1] - at, 128), BF16)
    span = TAPS * GROUP
    for pair in range(groups // 2):
        both = [
            (tap_terms(tall_ref, gz_ref, group) + dtaps_ref[group]) * scale for group in (2 * pair, 2 * pair + 1)
        ]
        both = jnp.concatenate(both, axis=0)
        both = jnp.concatenate([both, jnp.zeros((16, 128 - span), F32)], axis=1)
        half, place = divmod(pair, groups // 4)
        halves_ref[half, at + place * 16 : at + (place + 1) * 16, :] = both.astype(BF16)
    core = lax.axis_index("core")
    keep_ref[...] = halves_ref[core]
    send_ref[...] = halves_ref[1 - core]


def input_kernel(
    out_first_ref, out_inner_ref, out_second_ref, gz_first_ref, gz_inner_ref, gz_second_ref,
    halo_ref, g_ref, kernel_ref,
    out_ref, grad_ref, taps_ref, tall_ref,
):
    spread_taps(kernel_ref, taps_ref, True)
    low = is_low()
    rows = g_ref.shape[0]
    inner = rows - 2 * REACH
    tall_ref[pl.ds(rows * (1 - low), REACH)] = gz_second_ref[...]
    tall_ref[pl.ds(REACH * (2 - low), inner)] = gz_inner_ref[...]
    tall_ref[pl.ds(REACH + inner * low, REACH)] = gz_first_ref[...]
    tall_ref[pl.ds(rows * low, REACH)] = halo_ref[...]
    out_ref[REACH : REACH + inner] = out_inner_ref[...]
    out_ref[pl.ds((rows - REACH) * low, REACH)] = out_first_ref[...]
    out_ref[pl.ds((rows - REACH) * (1 - low), REACH)] = out_second_ref[...]

    def step(row, carry):
        at = row + REACH * low
        grad_ref[at] = (g_ref[at].astype(F32) + conv_row(tall_ref, taps_ref, row)).astype(BF16)
        return carry

    lax.fori_loop(0, rows - REACH, step, 0, unroll=True)


def input_rest_kernel(
    halo_ref, gz_first_ref, gz_inner_ref, gz_second_ref, g_ref, taps_ref, rest_ref,
    grad_ref, tall_ref, part_ref, sem,
):
    low = 1 - is_low()
    rows = g_ref.shape[0]
    inner = rows - 2 * REACH
    near = REACH - inner
    tall_ref[pl.ds(2 * REACH * low, REACH)] = halo_ref[...]
    tall_ref[REACH : 2 * REACH] = gz_second_ref[...]
    tall_ref[pl.ds(2 * REACH * (1 - low) + near * low, inner)] = gz_inner_ref[...]
    tall_ref[pl.ds((2 * REACH + inner) * (1 - low), near)] = gz_first_ref[pl.ds((REACH - near) * low, near)]
    first = (rows - REACH) * low

    def step(row, carry):
        part_ref[row] = (g_ref[first + row].astype(F32) + conv_row(tall_ref, taps_ref, row)).astype(BF16)
        return carry

    lax.fori_loop(0, REACH, step, 0, unroll=True)
    copy = pltpu.make_async_copy(part_ref, grad_ref.at[pl.ds(first, REACH)], sem)
    copy.start()
    copy.wait()


def final_kernel(mine_ref, other_ref, win_ref, woutt_ref, taps_ref, all_ref):
    core = lax.axis_index("core")
    quarter = 2 * lax.axis_index("x") + lax.axis_index("space") % 2
    chans, hidden_units = win_ref.shape
    size = mine_ref.shape[1]
    for turn in range(4):
        at = pl.ds(pl.multiple_of((quarter ^ turn) * size, 16), size)
        all_ref[core, at, :] = mine_ref[turn]
        all_ref[1 - core, at, :] = other_ref[turn]
    blocks = hidden_units // 128
    for index, ref in enumerate((win_ref, woutt_ref)):
        for block in range(blocks):
            ref[:, block * 128 : (block + 1) * 128] = all_ref[index, block * chans : (block + 1) * chans, :].astype(F32)
    groups = chans // GROUP
    for pair in range(groups // 2):
        half, place = divmod(pair, groups // 4)
        at = blocks * chans + place * 16
        both = all_ref[half, at : at + 16, :].astype(F32)
        for side in range(2):
            group = 2 * pair + side
            piece = both[side * 8 : side * 8 + 8]
            for tap in range(TAPS):
                taps_ref[tap, :, group * GROUP : (group + 1) * GROUP] = piece[:TAPS, tap * GROUP : (tap + 1) * GROUP]


def edge_kernel(x_ref, edge_ref, *, first):
    low = is_low() if first else 1 - is_low()
    edge_ref[...] = x_ref[pl.ds((x_ref.shape[0] - REACH) * low, REACH)]


PARAMS = pltpu.CompilerParams(vmem_limit_bytes=20 * 1024 * 1024)
SMALL = pltpu.CompilerParams(vmem_limit_bytes=8 * 1024 * 1024)
IN_VMEM = pl.BlockSpec(memory_space=pltpu.VMEM)


def swap(value, axis, mask):
    count = lax.axis_size(axis)
    return lax.ppermute(value, axis, [(source, source ^ mask) for source in range(count)])


def added(*terms):
    terms = [term.astype(F32) for term in terms]
    while len(terms) > 1:
        terms = [terms[at] + terms[at + 1] for at in range(0, len(terms), 2)]
    return terms[0].astype(BF16)


def on_device(
    features, dw_kernel, dw_bias, ln_gain, ln_bias, w_in, b_in, w_out, b_out, layer_scale, cotangent
):
    quarter = (2 * lax.axis_index("x") + lax.axis_index("space") % 2).astype(jnp.uint32)
    turns = [quarter ^ turn for turn in range(4)]
    features, *turns = lax.optimization_barrier((features, *turns))
    x = jnp.swapaxes(features[0, 0], 1, 2)
    g = jnp.swapaxes(cotangent[0, 0], 1, 2)
    rows, chans, width = x.shape
    hidden_units = w_in.shape[1]
    strips = lax.axis_size("space")
    narrow = jax.ShapeDtypeStruct((REACH, chans, width), BF16)
    image = jax.ShapeDtypeStruct((rows, chans, width), BF16)

    def edge(first):
        return pl.pallas_call(
            lambda *refs: edge_kernel(*refs, first=first),
            out_shape=narrow,
            in_specs=[IN_VMEM],
            out_specs=IN_VMEM,
            compiler_params=SMALL,
        )(x)

    def first_swap(value):
        return swap(value, "space", 1)

    def second_swap(value):
        pairs = [(low, low + 1) for low in range(1, strips - 1, 2)]
        return lax.ppermute(value, "space", pairs + [(high, low) for low, high in pairs])

    first_halo = first_swap(edge(True))
    devices = lax.axis_size("x") * lax.axis_size("core") * strips
    scale = float(devices * rows * width) ** (-0.5)
    groups = chans // GROUP
    span = TAPS * GROUP
    inner = rows - 2 * REACH

    tall = jax.ShapeDtypeStruct((3 * REACH, chans, width), BF16)

    def kept(count):
        small = jax.ShapeDtypeStruct((count, chans, width), BF16)
        large = jax.ShapeDtypeStruct((count, hidden_units, width), BF16)
        return (small, large, small, large)

    def scratch(shapes):
        return [pltpu.VMEM(shape.shape, shape.dtype) for shape in shapes]

    middle = jax.ShapeDtypeStruct((inner, chans, width), BF16)
    spread = jax.ShapeDtypeStruct((groups, span, 2 * span), BF16)
    matrix = jax.ShapeDtypeStruct((chans, hidden_units), F32)
    terms = (matrix, matrix, jax.ShapeDtypeStruct((groups, 8, span), F32))
    vectors = (dw_bias, ln_gain, ln_bias, b_out, layer_scale)
    across_lanes = jax.ShapeDtypeStruct((len(vectors), chans, 128), F32)
    hidden_lanes = jax.ShapeDtypeStruct((hidden_units, 128), F32)
    turned = jax.ShapeDtypeStruct((hidden_units, chans), BF16)
    taps, vectors, bias, w_in_t, w_out_turned = pl.pallas_call(
        prepare_kernel,
        out_shape=(spread, across_lanes, hidden_lanes, turned, turned),
        in_specs=[IN_VMEM] * (4 + len(vectors)),
        out_specs=(IN_VMEM,) * 5,
        compiler_params=SMALL,
    )(dw_kernel, w_in, w_out.T, b_in.reshape(-1, 128), *[vector[None] for vector in vectors])
    weights = (vectors, bias, w_in, w_in_t, w_out_turned, w_out.T)
    out_inner, gz_inner, *inner_terms = pl.pallas_call(
        inner_kernel,
        out_shape=(middle, middle, *terms),
        in_specs=[IN_VMEM] * 9,
        out_specs=(IN_VMEM,) * 5,
        scratch_shapes=scratch(kept(inner)),
        compiler_params=PARAMS,
    )(x, g, taps, *weights)
    second_edge, out_inner = lax.optimization_barrier((edge(False), out_inner))
    second_halo = second_swap(second_edge)
    half_rows = hidden_units // 128 * chans + groups // 2 * 8
    half_rows = (half_rows + 63) // 64 * 64
    half = jax.ShapeDtypeStruct((half_rows, 128), BF16)
    out_first, gz_first, *first_terms = pl.pallas_call(
        first_kernel,
        out_shape=(narrow, narrow, *terms),
        in_specs=[IN_VMEM] * 13,
        out_specs=(IN_VMEM,) * 5,
        scratch_shapes=scratch((tall, *kept(REACH))),
        compiler_params=PARAMS,
    )(x, first_halo, g, taps, *weights, *inner_terms)
    gz_first_halo = first_swap(gz_first)
    out_second, gz_second, *second_kept = pl.pallas_call(
        second_kernel,
        out_shape=(narrow, narrow, tall, *kept(REACH)),
        in_specs=[IN_VMEM] * 10,
        out_specs=(IN_VMEM,) * 7,
        compiler_params=PARAMS,
    )(x, second_halo, g, taps, *weights)
    gz_second_halo = second_swap(gz_second)
    keep, send = pl.pallas_call(
        lambda *refs: terms_kernel(*refs, scale=scale),
        out_shape=(half, half),
        in_specs=[IN_VMEM] * 9,
        out_specs=(IN_VMEM,) * 2,
        scratch_shapes=[pltpu.VMEM((2, half_rows, 128), BF16)],
        compiler_params=PARAMS,
    )(second_kept[0], gz_second, *second_kept[1:], *first_terms)
    keep, send, gz_first_halo = lax.optimization_barrier((keep, send, gz_first_halo))

    summed = added(keep, swap(send, "core", 1)).reshape(4, half_rows // 4, 128)

    def at(turn):
        return lax.dynamic_index_in_dim(summed, turns[turn], 0, keepdims=False)

    def partner(value, turn):
        return swap(value, ("x", "space"), (turn >> 1) * strips | (turn & 1))

    own = added(at(0), *[partner(at(turn), turn) for turn in (1, 2, 3)])
    out, grad_rest, back_taps = pl.pallas_call(
        input_kernel,
        out_shape=(image, image, spread),
        in_specs=[IN_VMEM] * 9,
        out_specs=(IN_VMEM,) * 3,
        scratch_shapes=[pltpu.VMEM((rows + REACH, chans, width), BF16)],
        compiler_params=PARAMS,
    )(out_first, out_inner, out_second, gz_first, gz_inner, gz_second, gz_first_halo, g, dw_kernel)
    bit = 2
    while bit < strips:
        masks = (bit, 2 * bit, 3 * bit) if 2 * bit < strips else (bit,)
        own = added(own, *[swap(own, "space", mask) for mask in masks])
        bit *= 4
    own, grad_rest = lax.optimization_barrier((own, grad_rest))
    mine = jnp.stack([own] + [partner(own, turn) for turn in (1, 2, 3)])
    grad_input = pl.pallas_call(
        input_rest_kernel,
        out_shape=image,
        in_specs=[IN_VMEM] * 6 + [pl.BlockSpec(memory_space=pl.ANY)],
        out_specs=pl.BlockSpec(memory_space=pl.ANY),
        scratch_shapes=[
            pltpu.VMEM((3 * REACH, chans, width), BF16),
            pltpu.VMEM((REACH, chans, width), BF16),
            pltpu.SemaphoreType.DMA(()),
        ],
        input_output_aliases={6: 0},
        compiler_params=PARAMS,
    )(gz_second_halo, gz_first, gz_inner, gz_second, g, back_taps, grad_rest)
    mine, grad_input = lax.optimization_barrier((mine, grad_input))
    other = swap(mine, "core", 1)
    grad_w_in, grad_w_out_t, grad_kernel = pl.pallas_call(
        final_kernel,
        out_shape=(matrix, matrix, jax.ShapeDtypeStruct((TAPS, TAPS, chans), F32)),
        in_specs=[IN_VMEM, IN_VMEM],
        out_specs=(IN_VMEM,) * 3,
        scratch_shapes=[pltpu.VMEM((2, half_rows, 128), BF16)],
        compiler_params=PARAMS,
    )(mine, other)
    block_output = jnp.swapaxes(out, 1, 2)[None, None]
    grad_image = jnp.swapaxes(grad_input, 1, 2)[None, None]
    return (block_output, grad_image, grad_w_in, grad_w_out_t.T, grad_kernel)


def solution(mesh):
    slides, strips = mesh.devices.shape
    split = Mesh(mesh.devices.reshape(slides // 2, 2, strips), ("x", "core", "space"))
    placed = P(("x", "core"), "space", None, None, None)
    return jax.shard_map(
        on_device,
        mesh=split,
        in_specs=(placed,) + (P(),) * 9 + (placed,),
        out_specs=(placed, placed, P(), P(), P()),
        check_vma=False,
    )
```
